32 devices in a mesh: rad: 4 (over y, x), azi: 8 (over z, core).
Axes of the slice: x: 2, y: 2, z: 4, core: 2. Of those that a mesh axis runs over, the one named last changes fastest.
Arguments:
- relative_base_heat: float32 [64, 256, 512], P('rad', 'azi'), may hold values from 0.75 to 1.25
- base_deformation_size: float32 [64, 256, 512], P('rad', 'azi'), may hold values from 0.25 to 1
- base_streamwise_flux: float32 [64, 256, 512], P('rad', 'azi'), may hold values from 0.2 to 1
- goal_heat_change: float32 [64, 256, 512], P('rad', 'azi'), may hold values from 0.25 to 2
- initial_costate_heat: float32 [64, 256, 512], P('rad', 'azi'), may hold values from 0.2 to 2
Outputs:
- temperature_adjoint: float32 [64, 256, 512], P('rad', 'azi')
- lengthwise_velocity_sensitivity: float32 [64, 256, 512], P('rad', 'azi')
The draws below stay inside these ranges and needn't reach their ends.
All inputs are finite; a program needn't handle non-finite values.
Results may differ from the reference program's by a relative error of at most 0.00045.
Values sent between devices are 32-bit elements; how exact they have to be, the bound alone decides.
A program may use at most 128 MiB of HBM per device.

```python
import math
import jax
import jax.numpy as jnp
from jax import lax

NRD = 16
STREAMWISE_CUTS = 512
THICKNESS_CUTS = 64
CIRCUMFERENTIAL = 256


def block_levels(own_key, extent, cuts, low, high):
    loudness, own = 1.0, jax.random.fold_in(own_key, 6)
    for position, blocks in cuts:
        steps = jnp.exp(jax.random.uniform(jax.random.fold_in(own, position), (blocks,), jnp.float32, low / len(cuts), high / len(cuts)))
        loudness = loudness * jnp.repeat(steps, extent[position] // blocks).reshape([-1 if axis == position else 1 for axis in range(len(extent))])
    return loudness


def setup_inputs(seed: int = 0) -> dict:
    streams_of = jax.random.split(jax.random.key(seed), 6)
    relative_base_heat = jnp.clip(0.75 + 0.5 * jax.random.uniform(streams_of[0], (THICKNESS_CUTS, CIRCUMFERENTIAL, STREAMWISE_CUTS), jnp.float32) ** block_levels(streams_of[0], (THICKNESS_CUTS, CIRCUMFERENTIAL, STREAMWISE_CUTS), ((0, 4), (1, 8)), -0.2, 0.2), 0.75, 1.25)
    base_deformation_size = jnp.clip(jnp.exp(math.log(1.0) - 1.3862944 * jax.random.uniform(streams_of[1], (THICKNESS_CUTS, CIRCUMFERENTIAL, STREAMWISE_CUTS), jnp.float32) ** block_levels(streams_of[1], (THICKNESS_CUTS, CIRCUMFERENTIAL, STREAMWISE_CUTS), ((0, 4), (1, 8)), -0.2, 0.2)), 0.25, 1.0)
    base_streamwise_flux = jnp.clip(0.2 + 0.8 * jax.random.uniform(streams_of[2], (THICKNESS_CUTS, CIRCUMFERENTIAL, STREAMWISE_CUTS), jnp.float32) ** block_levels(streams_of[2], (THICKNESS_CUTS, CIRCUMFERENTIAL, STREAMWISE_CUTS), ((0, 4), (1, 8)), -0.2, 0.2), 0.2, 1.0)
    goal_heat_change = jnp.clip(jnp.exp(math.log(2.0) - 2.0794415 * jax.random.uniform(streams_of[3], (THICKNESS_CUTS, CIRCUMFERENTIAL, STREAMWISE_CUTS), jnp.float32) ** block_levels(streams_of[3], (THICKNESS_CUTS, CIRCUMFERENTIAL, STREAMWISE_CUTS), ((0, 4), (1, 8)), -0.2, 0.2)), 0.25, 2.0)
    initial_costate_heat = jnp.clip(jnp.exp(math.log(2.0) - 2.3025851 * jax.random.uniform(streams_of[4], (THICKNESS_CUTS, CIRCUMFERENTIAL, STREAMWISE_CUTS), jnp.float32) ** block_levels(streams_of[4], (THICKNESS_CUTS, CIRCUMFERENTIAL, STREAMWISE_CUTS), ((0, 4), (1, 8)), -0.2, 0.2)), 0.2, 2.0)
    return {"relative_base_heat": relative_base_heat, "base_deformation_size": base_deformation_size, "base_streamwise_flux": base_streamwise_flux, "goal_heat_change": goal_heat_change, "initial_costate_heat": initial_costate_heat}


radial_weight = 8.0
azimuth_weight = 0.25
axial_weight = 0.25
flow_weight = 0.5
mass_weight = 1.0
heat_weight = 0.25
arrhenius_exponent = 2.0
slope_weight = 2.0


def line_geometry(first_row, number_lines_total, total_rows, segment_rows):
    row_int = jnp.arange(number_lines_total, dtype=jnp.int32) + first_row
    row_float = row_int.astype(jnp.float32)
    total_float = float(total_rows)
    segment_float = float(segment_rows)
    radius = 1.0 + (row_float + 0.5) / total_float
    inner_face = 1.0 + row_float / total_float
    outer_face = 1.0 + (row_float + 1.0) / total_float
    stiffness = radial_weight * segment_float * segment_float
    lower_off = jnp.where(row_int == 0, 0.0, -stiffness * inner_face / radius)
    upper_off = jnp.where(row_int == total_rows - 1, 0.0, -stiffness * outer_face / radius)
    radial_diag = stiffness * (inner_face + outer_face) / radius
    azimuth_coef = azimuth_weight / (radius * radius)
    return lower_off, upper_off, radial_diag, azimuth_coef


def plate_arrays(relative_base_heat, base_deformation_size, base_streamwise_flux):
    polymer_resistance = jnp.exp(-arrhenius_exponent * (relative_base_heat - 1.0))
    heating = heat_weight * arrhenius_exponent * polymer_resistance * base_deformation_size * base_deformation_size
    transport_factor = flow_weight * base_streamwise_flux
    extra_pivot_entry = mass_weight + 2.0 * axial_weight + transport_factor + heating
    return polymer_resistance, transport_factor, extra_pivot_entry


def explicit_rhs(old_center, side_sum, azimuth_coef, transport_factor, source_field):
    edge_nulls = jnp.zeros_like(old_center[:, :, :1])
    next_cell = jnp.concatenate([old_center[:, :, 1:], edge_nulls], axis=2)
    prev_cell = jnp.concatenate([edge_nulls, old_center[:, :, :-1]], axis=2)
    return (source_field + azimuth_coef[:, None, None] * side_sum + axial_weight * (prev_cell + next_cell)
            + transport_factor * next_cell + mass_weight * old_center)


def velocity_factor(relative_base_heat, polymer_resistance, base_deformation_size):
    edge_nulls = jnp.zeros_like(relative_base_heat[:, :, :1])
    resistance_derivative_array = jnp.concatenate([relative_base_heat[:, :, 1:] - relative_base_heat[:, :, :-1], edge_nulls], axis=2)
    return slope_weight * resistance_derivative_array - 2.0 * heat_weight * polymer_resistance * base_deformation_size


def thomas_lines(lower_off, diagonal, upper_off, right_side):
    def forward(carry_pair, row_items):
        running_g_term, running_h_term = carry_pair
        lower_row, diag_row, upper_row, right_row = row_items
        denominator = diag_row - lower_row * running_h_term
        new_g = (right_row - lower_row * running_g_term) / denominator
        new_h = upper_row / denominator
        return (new_g, new_h), (new_g, new_h)

    zero_plane = jnp.zeros_like(right_side[0])
    final_pair, eliminated = lax.scan(forward, (zero_plane, zero_plane), (lower_off, diagonal, upper_off, right_side))

    def backward(carry_next, row_items):
        solved_row = row_items[0] - row_items[1] * carry_next
        return solved_row, solved_row

    last_row, solved = lax.scan(backward, zero_plane, eliminated, reverse=True)
    return solved


def reference(relative_base_heat, base_deformation_size, base_streamwise_flux, goal_heat_change, initial_costate_heat):
    lower_off, upper_off, radial_diag, azimuth_coef = line_geometry(0, THICKNESS_CUTS, THICKNESS_CUTS, NRD)
    polymer_resistance, transport_factor, extra_pivot_entry = plate_arrays(relative_base_heat, base_deformation_size, base_streamwise_flux)
    diagonal = radial_diag[:, None, None] + 2.0 * azimuth_coef[:, None, None] + extra_pivot_entry
    sequence_ordinal = initial_costate_heat
    for sweep_index in range(2):
        side_sum = jnp.roll(sequence_ordinal, 1, axis=1) + jnp.roll(sequence_ordinal, -1, axis=1)
        right_side = explicit_rhs(sequence_ordinal, side_sum, azimuth_coef, transport_factor, goal_heat_change)
        sequence_ordinal = thomas_lines(lower_off, diagonal, upper_off, right_side)
    lengthwise_velocity_sensitivity = sequence_ordinal * velocity_factor(relative_base_heat, polymer_resistance, base_deformation_size)
    return sequence_ordinal, lengthwise_velocity_sensitivity
```

```python
import functools

import jax
import jax.numpy as jnp
from jax import lax
from jax.experimental import pallas as pl
from jax.experimental.pallas import tpu as pltpu
from jax.sharding import PartitionSpec as P

radial_weight = 8.0
azimuth_weight = 0.25
axial_weight = 0.25
flow_weight = 0.5
mass_weight = 1.0
heat_weight = 0.25
arrhenius_exponent = 2.0
slope_weight = 2.0

MESH = pl.DeviceIdType.MESH
LANES = 128
SUB = 8


def kernel(
    segments,
    sectors,
    heat_hbm,
    size_hbm,
    flux_hbm,
    goal_hbm,
    start_hbm,
    adjoint_hbm,
    sens_hbm,
    heat,
    size,
    flux,
    goal,
    state,
    inv,
    qa,
    rb,
    rhs,
    part,
    out_x,
    out_s,
    halo_out,
    halo_in,
    coef_out,
    coef_in,
    u_out,
    u_in,
    ret_out,
    ret_in,
    in_sem,
    out_sem,
    halo_ssem,
    halo_rsem,
    coef_ssem,
    coef_rsem,
    u_ssem,
    u_rsem,
    ret_ssem,
    ret_rsem,
):
    rows, width, axial = heat.shape
    groups = width // SUB
    chunks = axial // LANES
    per_chunk = segments // chunks
    tile_rows = width // per_chunk
    total = rows * segments
    stiffness = radial_weight * rows * rows

    seg = lax.axis_index("rad")
    sec = lax.axis_index("azi")
    above = lax.rem(sec + 1, sectors)
    below = lax.rem(sec + sectors - 1, sectors)
    peers = [lax.rem(seg + k, segments) for k in range(1, segments)]
    first = seg * rows

    loads = [
        pltpu.make_async_copy(src, dst, in_sem.at[n])
        for n, (src, dst) in enumerate(
            (
                (start_hbm, state),
                (heat_hbm, heat),
                (size_hbm, size),
                (flux_hbm, flux),
                (goal_hbm, goal),
            )
        )
    ]
    for load in loads:
        load.start()

    barrier = pltpu.get_barrier_semaphore()
    for peer in peers:
        pl.semaphore_signal(barrier, inc=1, device_id=(peer, sec), device_id_type=MESH)
    for near in (above, below):
        pl.semaphore_signal(barrier, inc=1, device_id=(seg, near), device_id_type=MESH)

    def halo_copies(sweep):
        return [
            pltpu.make_async_remote_copy(
                src_ref=halo_out.at[sweep, side],
                dst_ref=halo_in.at[sweep, side],
                send_sem=halo_ssem.at[sweep, side],
                recv_sem=halo_rsem.at[sweep, side],
                device_id=(seg, near),
                device_id_type=MESH,
            )
            for side, near in ((0, above), (1, below))
        ]

    def sends(src, dst, ssem, rsem):
        return [
            pltpu.make_async_remote_copy(
                src_ref=src.at[peer],
                dst_ref=dst.at[seg],
                send_sem=ssem.at[peer],
                recv_sem=rsem.at[seg],
                device_id=(peer, sec),
                device_id_type=MESH,
            )
            for peer in peers
        ]

    def await_from(src, dst, ssem, rsem):
        for peer in peers:
            pltpu.make_async_remote_copy(
                src_ref=src.at[peer],
                dst_ref=dst.at[peer],
                send_sem=ssem.at[peer],
                recv_sem=rsem.at[peer],
                device_id=(peer, sec),
                device_id_type=MESH,
            ).wait_recv()

    def geometry(i):
        row = (first + i).astype(jnp.float32)
        radius = 1.0 + (row + 0.5) * (1.0 / total)
        low = stiffness * (1.0 + row * (1.0 / total))
        high = stiffness * (1.0 + (row + 1.0) * (1.0 / total))
        return radius, low, high

    def azimuth_coef(radius):
        return azimuth_weight / jnp.full((1, LANES), radius, jnp.float32)

    def wide(line):
        return jnp.concatenate([line] * chunks, axis=1)

    loads[0].wait()

    def pack(i, carry):
        halo_out[0, 0, pl.ds(i, 1), :] = state[i, width - 1 : width, :]
        halo_out[0, 1, pl.ds(i, 1), :] = state[i, 0:1, :]
        return carry

    lax.fori_loop(0, rows, pack, 0, unroll=4)
    pl.semaphore_wait(barrier, segments + 1)
    halos = halo_copies(0)
    for copy in halos:
        copy.start()

    for load in loads[1:4]:
        load.wait()

    def pieces():
        for c in range(chunks):
            for k in range(per_chunk):
                yield c * per_chunk + k, slice(k * tile_rows, (k + 1) * tile_rows), c

    def scatter(ref, slot, plane, c_first, c_last):
        for owner, where_rows, c in pieces():
            if c_first <= c < c_last:
                at = (c - c_first) * LANES
                ref[owner, slot] = plane[where_rows, at : at + LANES]

    half = 2 * LANES
    for h in range(axial // half):
        cols = slice(h * half, (h + 1) * half)

        def eliminate(i, carry):
            ratio, ea, prod, va, _ = carry
            radius, low, high = geometry(i)
            az2 = 2.0 * azimuth_coef(radius)
            az2 = jnp.concatenate([az2, az2], axis=1)
            viscosity = jnp.exp(
                arrhenius_exponent - arrhenius_exponent * heat[i, :, cols]
            )
            extent = size[i, :, cols]
            shear = (heat_weight * arrhenius_exponent) * viscosity * extent
            ahead = radius * (axial_weight + flow_weight * flux[i, :, cols])
            excess = (
                ahead + radius * (shear * extent + (mass_weight + axial_weight)) + az2
            )
            top = low * ratio + excess
            inverse = 1.0 / (top + high)
            ratio = top * inverse
            ea = (low * inverse) * ea
            upper = high * inverse
            va = va + prod * ea
            prod = prod * upper
            flux[i, :, cols] = ahead
            size[i, :, cols] = shear
            inv[i, :, cols] = inverse
            qa[i, :, cols] = ea
            return ratio, ea, prod, va, upper

        one = jnp.ones((width, half), jnp.float32)
        zero = jnp.zeros((width, half), jnp.float32)
        _, ea, _, va, upper = lax.fori_loop(
            0, rows, eliminate, (one, one, one, zero, zero)
        )
        scatter(coef_out, 0, va, 2 * h, 2 * h + 2)
        scatter(coef_out, 1, ea, 2 * h, 2 * h + 2)
        scatter(coef_out, 2, upper, 2 * h, 2 * h + 2)

    coef_sends = sends(coef_out, coef_in, coef_ssem, coef_rsem)
    for copy in coef_sends:
        copy.start()
    coef_in[seg] = coef_out[seg]

    def respond(n, carry):
        q_next, r_next = carry
        i = rows - 1 - n
        _, _, high = geometry(i)
        upper = high * inv[i]
        q_next = qa[i] + upper * q_next
        r_next = upper * r_next
        qa[i] = q_next
        rb[i] = r_next
        return q_next, r_next

    lax.fori_loop(
        0,
        rows,
        respond,
        (jnp.zeros((width, axial), jnp.float32), jnp.ones((width, axial), jnp.float32)),
    )

    loads[4].wait()
    sub = lax.broadcasted_iota(jnp.int32, (SUB, axial), 0)
    lane = lax.broadcasted_iota(jnp.int32, (SUB, axial), 1)

    def right_side(sweep, chosen):
        def step(i, carry):
            radius, _, _ = geometry(i)
            az = wide(azimuth_coef(radius))
            rolled_up, rolled_down, new = {}, {}, []

            def block(g):
                return state[i, g * SUB : (g + 1) * SUB, :]

            def up(g):
                if g < 0:
                    return jnp.broadcast_to(
                        halo_in[sweep, 0, pl.ds(i, 1), :], (SUB, axial)
                    )
                if g not in rolled_up:
                    rolled_up[g] = pltpu.roll(block(g), 1, 0)
                return rolled_up[g]

            def down(g):
                if g >= groups:
                    return jnp.broadcast_to(
                        halo_in[sweep, 1, pl.ds(i, 1), :], (SUB, axial)
                    )
                if g not in rolled_down:
                    rolled_down[g] = pltpu.roll(block(g), SUB - 1, 0)
                return rolled_down[g]

            for g, (u_first, u_last) in zip(chosen, carry):
                here = slice(g * SUB, (g + 1) * SUB)
                x = block(g)
                sides = jnp.where(sub == 0, up(g - 1), up(g)) + jnp.where(
                    sub == SUB - 1, down(g + 1), down(g)
                )
                before = jnp.where(lane == 0, 0.0, pltpu.roll(x, 1, 1))
                after = jnp.where(lane == axial - 1, 0.0, pltpu.roll(x, axial - 1, 1))
                value = (
                    radius * (goal[i, here, :] + mass_weight * x + axial_weight * before)
                    + flux[i, here, :] * after
                    + az * sides
                )
                rhs[i, here, :] = value
                new.append(
                    (u_first + qa[i, here, :] * value, u_last + rb[i, here, :] * value)
                )
            return tuple(new)

        zero = jnp.zeros((SUB, axial), jnp.float32)
        sums = lax.fori_loop(0, rows, step, tuple((zero, zero) for _ in chosen))
        for g, pair in zip(chosen, sums):
            for slot, plane in enumerate(pair):
                for owner, where_rows, c in pieces():
                    at = g * SUB - where_rows.start
                    if 0 <= at < tile_rows:
                        u_out[sweep, owner, slot, at : at + SUB, :] = plane[
                            :, c * LANES : (c + 1) * LANES
                        ]

    def send_ends(sweep):
        copies = sends(
            u_out.at[sweep], u_in.at[sweep], u_ssem.at[sweep], u_rsem.at[sweep]
        )
        for copy in copies:
            copy.start()
        u_in[sweep, seg] = u_out[sweep, seg]
        return copies

    def await_ends(sweep):
        await_from(u_out.at[sweep], u_in.at[sweep], u_ssem.at[sweep], u_rsem.at[sweep])

    def substitute():
        def forward(i, g):
            _, low, _ = geometry(i)
            g = inv[i] * (rhs[i] + low * g)
            rhs[i] = g
            return g

        def backward(n, p):
            i = rows - 1 - n
            _, _, high = geometry(i)
            p = rhs[i] + (high * inv[i]) * p
            part[i] = p
            return p

        zero = jnp.zeros((width, axial), jnp.float32)
        lax.fori_loop(0, rows, forward, zero)
        lax.fori_loop(0, rows, backward, zero)

    def reduced_factors():
        factors, beta = [], None
        for s in range(segments):
            v_first, v_last, w_last = coef_in[s, 0], coef_in[s, 1], coef_in[s, 2]
            w_first = v_last * ((segments + s + 1.0) / (segments + s))
            if s == 0:
                factors.append((None, None, None, w_first, w_last, None))
                beta = w_last
                continue
            scale = 1.0 / (1.0 - v_first * beta)
            q = scale * w_first
            cross = v_last * beta
            new_beta = w_last + cross * q
            factors.append((scale, scale * v_first, v_last, q, new_beta, cross))
            beta = new_beta
        return factors

    def reduced_solve(sweep, factors):
        firsts, lasts = [], []
        for s in range(segments):
            u_first = u_in[sweep, s, 0] * (segments / (stiffness * (segments + s)))
            u_last = u_in[sweep, s, 1] * (segments / (stiffness * (segments + s + 1)))
            if s == 0:
                firsts.append(u_first)
                lasts.append(u_last)
                continue
            scale, scaled_v, v_last, _, _, cross = factors[s]
            p = scale * u_first + scaled_v * lasts[s - 1]
            firsts.append(p)
            lasts.append(u_last + v_last * lasts[s - 1] + cross * p)
        blank = jnp.zeros((tile_rows, LANES), jnp.float32)
        beyond = blank
        ret_out[sweep, 0, 0] = blank
        for s in range(segments - 1, -1, -1):
            ret_out[sweep, s, 1] = beyond
            if s < segments - 1:
                ret_out[sweep, s + 1, 0] = lasts[s] + factors[s][4] * beyond
            beyond = firsts[s] + factors[s][3] * beyond if s > 0 else beyond

    def send_back(sweep):
        copies = sends(
            ret_out.at[sweep], ret_in.at[sweep], ret_ssem.at[sweep], ret_rsem.at[sweep]
        )
        for copy in copies:
            copy.start()
        ret_in[sweep, seg] = ret_out[sweep, seg]
        return copies

    def await_back(sweep):
        await_from(
            ret_out.at[sweep], ret_in.at[sweep], ret_ssem.at[sweep], ret_rsem.at[sweep]
        )

    def ends(sweep):
        planes = []
        for slot in range(2):
            planes.append(
                jnp.concatenate(
                    [
                        jnp.concatenate(
                            [
                                ret_in[sweep, c * per_chunk + k, slot]
                                for k in range(per_chunk)
                            ],
                            axis=0,
                        )
                        for c in range(chunks)
                    ],
                    axis=1,
                )
            )
        return planes

    for copy in halos:
        copy.wait_recv()
    right_side(0, tuple(range(groups)))
    started = [coef_sends, halos, send_ends(0)]
    substitute()
    await_from(coef_out, coef_in, coef_ssem, coef_rsem)
    factors = reduced_factors()
    await_ends(0)
    reduced_solve(0, factors)
    started.append(send_back(0))

    last_lane = lax.broadcasted_iota(jnp.int32, (width, axial), 1) == axial - 1

    def slope(i, carry):
        here = heat[i]
        rise = jnp.where(last_lane, 0.0, pltpu.roll(here, axial - 1, 1) - here)
        heat[i] = slope_weight * rise - size[i]
        return carry

    lax.fori_loop(0, rows, slope, 0)

    await_back(0)
    a, b = ends(0)

    def advance(i, carry):
        x = part[i] + qa[i] * a + rb[i] * b
        state[i] = x
        halo_out[1, 0, pl.ds(i, 1), :] = x[width - 1 : width, :]
        halo_out[1, 1, pl.ds(i, 1), :] = x[0:1, :]
        return carry

    lax.fori_loop(0, rows, advance, 0)
    halos = halo_copies(1)
    for copy in halos:
        copy.start()

    for copy in halos:
        copy.wait_recv()
    right_side(1, tuple(range(groups)))
    started += [halos, send_ends(1)]
    substitute()
    await_ends(1)
    reduced_solve(1, reduced_factors())
    started.append(send_back(1))
    await_back(1)
    a, b = ends(1)

    quarter = rows // 4
    stores = []
    for n in range(4):

        def finish(i, carry):
            x = part[i] + qa[i] * a + rb[i] * b
            out_x[i] = x
            out_s[i] = x * heat[i]
            return carry

        lax.fori_loop(n * quarter, (n + 1) * quarter, finish, 0)
        span = slice(n * quarter, (n + 1) * quarter)
        for m, (src, dst) in enumerate(((out_x, adjoint_hbm), (out_s, sens_hbm))):
            store = pltpu.make_async_copy(
                src.at[pl.ds(n * quarter, quarter)],
                dst.at[pl.ds(n * quarter, quarter)],
                out_sem.at[m, n],
            )
            store.start()
            stores.append(store)

    for copies in started:
        for copy in copies:
            copy.wait_send()
    for store in stores:
        store.wait()


def solution(mesh):
    segments, sectors = mesh.shape["rad"], mesh.shape["azi"]
    spec = P("rad", "azi", None)

    def body(heat, size, flux, goal, start):
        rows, width, axial = heat.shape
        tile_rows = width * axial // (segments * LANES)
        block = pltpu.VMEM((rows, width, axial), jnp.float32)
        tile = (tile_rows, LANES)
        shape = jax.ShapeDtypeStruct((rows, width, axial), jnp.float32)
        dma = pltpu.SemaphoreType.DMA
        cells = rows * width * axial
        return pl.pallas_call(
            functools.partial(kernel, segments, sectors),
            out_shape=(shape, shape),
            in_specs=[pl.BlockSpec(memory_space=pl.ANY)] * 5,
            out_specs=[pl.BlockSpec(memory_space=pl.ANY)] * 2,
            scratch_shapes=[block] * 12
            + [
                pltpu.VMEM((2, 2, rows, axial), jnp.float32),
                pltpu.VMEM((2, 2, rows, axial), jnp.float32),
                pltpu.VMEM((segments, 3) + tile, jnp.float32),
                pltpu.VMEM((segments, 3) + tile, jnp.float32),
                pltpu.VMEM((2, segments, 2) + tile, jnp.float32),
                pltpu.VMEM((2, segments, 2) + tile, jnp.float32),
                pltpu.VMEM((2, segments, 2) + tile, jnp.float32),
                pltpu.VMEM((2, segments, 2) + tile, jnp.float32),
                dma((5,)),
                dma((2, 4)),
                dma((2, 2)),
                dma((2, 2)),
                dma((segments,)),
                dma((segments,)),
                dma((2, segments)),
                dma((2, segments)),
                dma((2, segments)),
                dma((2, segments)),
            ],
            compiler_params=pltpu.CompilerParams(
                collective_id=0, has_side_effects=True, vmem_limit_bytes=32 * 2**20
            ),
            cost_estimate=pl.CostEstimate(
                flops=120 * cells, bytes_accessed=28 * cells, transcendentals=2 * cells
            ),
        )(heat, size, flux, goal, start)

    return jax.shard_map(
        body, mesh=mesh, in_specs=(spec,) * 5, out_specs=(spec, spec), check_vma=False
    )
```

```python
import functools

import jax
import jax.numpy as jnp
from jax import lax
from jax.experimental import pallas as pl
from jax.experimental.pallas import tpu as pltpu
from jax.sharding import PartitionSpec as P

radial_weight = 8.0
azimuth_weight = 0.25
axial_weight = 0.25
flow_weight = 0.5
mass_weight = 1.0
heat_weight = 0.25
arrhenius_exponent = 2.0
slope_weight = 2.0

MESH = pl.DeviceIdType.MESH
LANES = 128
SUB = 8


def kernel(
    segments,
    sectors,
    heat_hbm,
    size_hbm,
    flux_hbm,
    goal_hbm,
    start_hbm,
    adjoint_hbm,
    sens_hbm,
    heat,
    size,
    flux,
    goal,
    state,
    inv,
    qa,
    rb,
    rhs,
    part,
    out_x,
    out_s,
    halo_out,
    halo_in,
    coef_out,
    coef_in,
    u_out,
    u_in,
    ret_out,
    ret_in,
    in_sem,
    out_sem,
    halo_ssem,
    halo_rsem,
    coef_ssem,
    coef_rsem,
    u_ssem,
    u_rsem,
    ret_ssem,
    ret_rsem,
):
    rows, width, axial = heat.shape
    groups = width // SUB
    chunks = axial // LANES
    per_chunk = segments // chunks
    tile_rows = width // per_chunk
    total = rows * segments
    stiffness = radial_weight * rows * rows

    seg = lax.axis_index("rad")
    sec = lax.axis_index("azi")
    above = lax.rem(sec + 1, sectors)
    below = lax.rem(sec + sectors - 1, sectors)
    peers = [lax.rem(seg + k, segments) for k in range(1, segments)]
    first = seg * rows

    span = rows // 2
    loads = [
        [
            pltpu.make_async_copy(
                src.at[pl.ds(part_of * span, span)],
                dst.at[pl.ds(part_of * span, span)],
                in_sem.at[n, part_of],
            )
            for part_of in range(2)
        ]
        for n, (src, dst) in enumerate(
            (
                (start_hbm, state),
                (heat_hbm, heat),
                (size_hbm, size),
                (flux_hbm, flux),
                (goal_hbm, goal),
            )
        )
    ]
    for load in loads:
        for copy in load:
            copy.start()

    def await_load(load):
        for copy in load:
            copy.wait()

    barrier = pltpu.get_barrier_semaphore()
    for peer in peers:
        pl.semaphore_signal(barrier, inc=1, device_id=(peer, sec), device_id_type=MESH)
    for near in (above, below):
        pl.semaphore_signal(barrier, inc=1, device_id=(seg, near), device_id_type=MESH)

    def halo_copies(sweep):
        return [
            pltpu.make_async_remote_copy(
                src_ref=halo_out.at[sweep, side],
                dst_ref=halo_in.at[sweep, side],
                send_sem=halo_ssem.at[sweep, side],
                recv_sem=halo_rsem.at[sweep, side],
                device_id=(seg, near),
                device_id_type=MESH,
            )
            for side, near in ((0, above), (1, below))
        ]

    def sends(src, dst, ssem, rsem):
        return [
            pltpu.make_async_remote_copy(
                src_ref=src.at[peer],
                dst_ref=dst.at[seg],
                send_sem=ssem.at[peer],
                recv_sem=rsem.at[seg],
                device_id=(peer, sec),
                device_id_type=MESH,
            )
            for peer in peers
        ]

    def await_from(src, dst, ssem, rsem):
        for peer in peers:
            pltpu.make_async_remote_copy(
                src_ref=src.at[peer],
                dst_ref=dst.at[peer],
                send_sem=ssem.at[peer],
                recv_sem=rsem.at[peer],
                device_id=(peer, sec),
                device_id_type=MESH,
            ).wait_recv()

    def geometry(i):
        row = (first + i).astype(jnp.float32)
        radius = 1.0 + (row + 0.5) * (1.0 / total)
        low = stiffness * (1.0 + row * (1.0 / total))
        high = stiffness * (1.0 + (row + 1.0) * (1.0 / total))
        return radius, low, high

    def azimuth_coef(radius):
        return azimuth_weight / jnp.full((1, LANES), radius, jnp.float32)

    def wide(line):
        return jnp.concatenate([line] * chunks, axis=1)

    await_load(loads[0])

    def pack(i, carry):
        halo_out[0, 0, pl.ds(i, 1), :] = state[i, width - 1 : width, :]
        halo_out[0, 1, pl.ds(i, 1), :] = state[i, 0:1, :]
        return carry

    lax.fori_loop(0, rows, pack, 0, unroll=4)
    pl.semaphore_wait(barrier, segments + 1)
    halos = halo_copies(0)
    for copy in halos:
        copy.start()

    for load in loads[1:4]:
        await_load(load)

    def pieces():
        for c in range(chunks):
            for k in range(per_chunk):
                yield c * per_chunk + k, slice(k * tile_rows, (k + 1) * tile_rows), c

    def scatter(ref, slot, plane, c_first, c_last):
        for owner, where_rows, c in pieces():
            if c_first <= c < c_last:
                at = (c - c_first) * LANES
                ref[owner, slot] = plane[where_rows, at : at + LANES]

    half = 2 * LANES
    for h in range(axial // half):
        cols = slice(h * half, (h + 1) * half)

        def eliminate(i, carry):
            ratio, ea, prod, va, _ = carry
            radius, low, high = geometry(i)
            az2 = 2.0 * azimuth_coef(radius)
            az2 = jnp.concatenate([az2, az2], axis=1)
            viscosity = jnp.exp(
                arrhenius_exponent - arrhenius_exponent * heat[i, :, cols]
            )
            extent = size[i, :, cols]
            shear = (heat_weight * arrhenius_exponent) * viscosity * extent
            ahead = radius * (axial_weight + flow_weight * flux[i, :, cols])
            excess = (
                ahead + radius * (shear * extent + (mass_weight + axial_weight)) + az2
            )
            top = low * ratio + excess
            inverse = 1.0 / (top + high)
            ratio = top * inverse
            ea = (low * inverse) * ea
            upper = high * inverse
            va = va + prod * ea
            prod = prod * upper
            flux[i, :, cols] = ahead
            size[i, :, cols] = shear
            inv[i, :, cols] = inverse
            qa[i, :, cols] = ea
            return ratio, ea, prod, va, upper

        one = jnp.ones((width, half), jnp.float32)
        zero = jnp.zeros((width, half), jnp.float32)
        _, ea, _, va, upper = lax.fori_loop(
            0, rows, eliminate, (one, one, one, zero, zero)
        )
        scatter(coef_out, 0, va, 2 * h, 2 * h + 2)
        scatter(coef_out, 1, ea, 2 * h, 2 * h + 2)
        scatter(coef_out, 2, upper, 2 * h, 2 * h + 2)

    coef_sends = sends(coef_out, coef_in, coef_ssem, coef_rsem)
    for copy in coef_sends:
        copy.start()
    coef_in[seg] = coef_out[seg]

    def respond(n, carry):
        q_next, r_next = carry
        i = rows - 1 - n
        _, _, high = geometry(i)
        upper = high * inv[i]
        q_next = qa[i] + upper * q_next
        r_next = upper * r_next
        qa[i] = q_next
        rb[i] = r_next
        return q_next, r_next

    lax.fori_loop(
        0,
        rows,
        respond,
        (jnp.zeros((width, axial), jnp.float32), jnp.ones((width, axial), jnp.float32)),
    )

    await_load(loads[4])
    sub = lax.broadcasted_iota(jnp.int32, (SUB, axial), 0)
    lane = lax.broadcasted_iota(jnp.int32, (SUB, axial), 1)

    def right_side(sweep, chosen):
        def step(i, carry):
            radius, _, _ = geometry(i)
            az = wide(azimuth_coef(radius))
            rolled_up, rolled_down, new = {}, {}, []

            def block(g):
                return state[i, g * SUB : (g + 1) * SUB, :]

            def up(g):
                if g < 0:
                    return jnp.broadcast_to(
                        halo_in[sweep, 0, pl.ds(i, 1), :], (SUB, axial)
                    )
                if g not in rolled_up:
                    rolled_up[g] = pltpu.roll(block(g), 1, 0)
                return rolled_up[g]

            def down(g):
                if g >= groups:
                    return jnp.broadcast_to(
                        halo_in[sweep, 1, pl.ds(i, 1), :], (SUB, axial)
                    )
                if g not in rolled_down:
                    rolled_down[g] = pltpu.roll(block(g), SUB - 1, 0)
                return rolled_down[g]

            for g, (u_first, u_last) in zip(chosen, carry):
                here = slice(g * SUB, (g + 1) * SUB)
                x = block(g)
                sides = jnp.where(sub == 0, up(g - 1), up(g)) + jnp.where(
                    sub == SUB - 1, down(g + 1), down(g)
                )
                before = jnp.where(lane == 0, 0.0, pltpu.roll(x, 1, 1))
                after = jnp.where(lane == axial - 1, 0.0, pltpu.roll(x, axial - 1, 1))
                value = (
                    radius * (goal[i, here, :] + mass_weight * x + axial_weight * before)
                    + flux[i, here, :] * after
                    + az * sides
                )
                rhs[i, here, :] = value
                new.append(
                    (u_first + qa[i, here, :] * value, u_last + rb[i, here, :] * value)
                )
            return tuple(new)

        zero = jnp.zeros((SUB, axial), jnp.float32)
        sums = lax.fori_loop(0, rows, step, tuple((zero, zero) for _ in chosen))
        for g, pair in zip(chosen, sums):
            for slot, plane in enumerate(pair):
                for owner, where_rows, c in pieces():
                    at = g * SUB - where_rows.start
                    if 0 <= at < tile_rows:
                        u_out[sweep, owner, slot, at : at + SUB, :] = plane[
                            :, c * LANES : (c + 1) * LANES
                        ]

    def send_ends(sweep):
        copies = sends(
            u_out.at[sweep], u_in.at[sweep], u_ssem.at[sweep], u_rsem.at[sweep]
        )
        for copy in copies:
            copy.start()
        u_in[sweep, seg] = u_out[sweep, seg]
        return copies

    def await_ends(sweep):
        await_from(u_out.at[sweep], u_in.at[sweep], u_ssem.at[sweep], u_rsem.at[sweep])

    def substitute():
        def forward(i, g):
            _, low, _ = geometry(i)
            g = inv[i] * (rhs[i] + low * g)
            rhs[i] = g
            return g

        def backward(n, p):
            i = rows - 1 - n
            _, _, high = geometry(i)
            p = rhs[i] + (high * inv[i]) * p
            part[i] = p
            return p

        zero = jnp.zeros((width, axial), jnp.float32)
        lax.fori_loop(0, rows, forward, zero)
        lax.fori_loop(0, rows, backward, zero)

    def reduced_factors():
        factors, beta = [], None
        for s in range(segments):
            v_first, v_last, w_last = coef_in[s, 0], coef_in[s, 1], coef_in[s, 2]
            w_first = v_last * ((segments + s + 1.0) / (segments + s))
            if s == 0:
                factors.append((None, None, None, w_first, w_last, None))
                beta = w_last
                continue
            scale = 1.0 / (1.0 - v_first * beta)
            q = scale * w_first
            cross = v_last * beta
            new_beta = w_last + cross * q
            factors.append((scale, scale * v_first, v_last, q, new_beta, cross))
            beta = new_beta
        return factors

    def reduced_solve(sweep, factors):
        firsts, lasts = [], []
        for s in range(segments):
            u_first = u_in[sweep, s, 0] * (segments / (stiffness * (segments + s)))
            u_last = u_in[sweep, s, 1] * (segments / (stiffness * (segments + s + 1)))
            if s == 0:
                firsts.append(u_first)
                lasts.append(u_last)
                continue
            scale, scaled_v, v_last, _, _, cross = factors[s]
            p = scale * u_first + scaled_v * lasts[s - 1]
            firsts.append(p)
            lasts.append(u_last + v_last * lasts[s - 1] + cross * p)
        blank = jnp.zeros((tile_rows, LANES), jnp.float32)
        beyond = blank
        ret_out[sweep, 0, 0] = blank
        for s in range(segments - 1, -1, -1):
            ret_out[sweep, s, 1] = beyond
            if s < segments - 1:
                ret_out[sweep, s + 1, 0] = lasts[s] + factors[s][4] * beyond
            beyond = firsts[s] + factors[s][3] * beyond if s > 0 else beyond

    def send_back(sweep):
        copies = sends(
            ret_out.at[sweep], ret_in.at[sweep], ret_ssem.at[sweep], ret_rsem.at[sweep]
        )
        for copy in copies:
            copy.start()
        ret_in[sweep, seg] = ret_out[sweep, seg]
        return copies

    def await_back(sweep):
        await_from(
            ret_out.at[sweep], ret_in.at[sweep], ret_ssem.at[sweep], ret_rsem.at[sweep]
        )

    def ends(sweep):
        planes = []
        for slot in range(2):
            planes.append(
                jnp.concatenate(
                    [
                        jnp.concatenate(
                            [
                                ret_in[sweep, c * per_chunk + k, slot]
                                for k in range(per_chunk)
                            ],
                            axis=0,
                        )
                        for c in range(chunks)
                    ],
                    axis=1,
                )
            )
        return planes

    for copy in halos:
        copy.wait_recv()
    right_side(0, tuple(range(groups)))
    started = [coef_sends, halos, send_ends(0)]
    substitute()
    await_from(coef_out, coef_in, coef_ssem, coef_rsem)
    factors = reduced_factors()
    await_ends(0)
    reduced_solve(0, factors)
    started.append(send_back(0))

    last_lane = lax.broadcasted_iota(jnp.int32, (width, axial), 1) == axial - 1

    def slope(i, carry):
        here = heat[i]
        rise = jnp.where(last_lane, 0.0, pltpu.roll(here, axial - 1, 1) - here)
        heat[i] = slope_weight * rise - size[i]
        return carry

    lax.fori_loop(0, rows, slope, 0)

    await_back(0)
    a, b = ends(0)

    def advance(i, carry):
        x = part[i] + qa[i] * a + rb[i] * b
        state[i] = x
        halo_out[1, 0, pl.ds(i, 1), :] = x[width - 1 : width, :]
        halo_out[1, 1, pl.ds(i, 1), :] = x[0:1, :]
        return carry

    lax.fori_loop(0, rows, advance, 0)
    halos = halo_copies(1)
    for copy in halos:
        copy.start()

    for copy in halos:
        copy.wait_recv()
    right_side(1, tuple(range(groups)))
    started += [halos, send_ends(1)]
    substitute()
    await_ends(1)
    reduced_solve(1, reduced_factors())
    started.append(send_back(1))
    await_back(1)
    a, b = ends(1)

    quarter = rows // 4
    stores = []
    for n in range(4):

        def finish(i, carry):
            x = part[i] + qa[i] * a + rb[i] * b
            out_x[i] = x
            out_s[i] = x * heat[i]
            return carry

        lax.fori_loop(n * quarter, (n + 1) * quarter, finish, 0)
        span = slice(n * quarter, (n + 1) * quarter)
        for m, (src, dst) in enumerate(((out_x, adjoint_hbm), (out_s, sens_hbm))):
            store = pltpu.make_async_copy(
                src.at[pl.ds(n * quarter, quarter)],
                dst.at[pl.ds(n * quarter, quarter)],
                out_sem.at[m, n],
            )
            store.start()
            stores.append(store)

    for copies in started:
        for copy in copies:
            copy.wait_send()
    for store in stores:
        store.wait()


def solution(mesh):
    segments, sectors = mesh.shape["rad"], mesh.shape["azi"]
    spec = P("rad", "azi", None)

    def body(heat, size, flux, goal, start):
        rows, width, axial = heat.shape
        tile_rows = width * axial // (segments * LANES)
        block = pltpu.VMEM((rows, width, axial), jnp.float32)
        tile = (tile_rows, LANES)
        shape = jax.ShapeDtypeStruct((rows, width, axial), jnp.float32)
        dma = pltpu.SemaphoreType.DMA
        cells = rows * width * axial
        return pl.pallas_call(
            functools.partial(kernel, segments, sectors),
            out_shape=(shape, shape),
            in_specs=[pl.BlockSpec(memory_space=pltpu.HBM)] * 5,
            out_specs=[pl.BlockSpec(memory_space=pl.ANY)] * 2,
            scratch_shapes=[block] * 12
            + [
                pltpu.VMEM((2, 2, rows, axial), jnp.float32),
                pltpu.VMEM((2, 2, rows, axial), jnp.float32),
                pltpu.VMEM((segments, 3) + tile, jnp.float32),
                pltpu.VMEM((segments, 3) + tile, jnp.float32),
                pltpu.VMEM((2, segments, 2) + tile, jnp.float32),
                pltpu.VMEM((2, segments, 2) + tile, jnp.float32),
                pltpu.VMEM((2, segments, 2) + tile, jnp.float32),
                pltpu.VMEM((2, segments, 2) + tile, jnp.float32),
                dma((5, 2)),
                dma((2, 4)),
                dma((2, 2)),
                dma((2, 2)),
                dma((segments,)),
                dma((segments,)),
                dma((2, segments)),
                dma((2, segments)),
                dma((2, segments)),
                dma((2, segments)),
            ],
            compiler_params=pltpu.CompilerParams(
                collective_id=0, has_side_effects=True, vmem_limit_bytes=32 * 2**20
            ),
            cost_estimate=pl.CostEstimate(
                flops=120 * cells, bytes_accessed=28 * cells, transcendentals=2 * cells
            ),
        )(heat, size, flux, goal, start)

    return jax.shard_map(
        body, mesh=mesh, in_specs=(spec,) * 5, out_specs=(spec, spec), check_vma=False
    )
```

```python
import functools

import jax
import jax.numpy as jnp
from jax import lax
from jax.experimental import pallas as pl
from jax.experimental.pallas import tpu as pltpu
from jax.sharding import PartitionSpec as P

radial_weight = 8.0
azimuth_weight = 0.25
axial_weight = 0.25
flow_weight = 0.5
mass_weight = 1.0
heat_weight = 0.25
arrhenius_exponent = 2.0
slope_weight = 2.0

MESH = pl.DeviceIdType.MESH
LANES = 128
SUB = 8


def kernel(
    segments,
    sectors,
    heat_hbm,
    size_hbm,
    flux_hbm,
    goal_hbm,
    start_hbm,
    adjoint_hbm,
    sens_hbm,
    heat,
    size,
    flux,
    goal,
    state,
    inv,
    qa,
    rb,
    rhs,
    part,
    out_x,
    out_s,
    halo_out,
    halo_in,
    coef_out,
    coef_in,
    u_out,
    u_in,
    ret_out,
    ret_in,
    in_sem,
    out_sem,
    halo_ssem,
    halo_rsem,
    coef_ssem,
    coef_rsem,
    u_ssem,
    u_rsem,
    ret_ssem,
    ret_rsem,
):
    rows, width, axial = heat.shape
    groups = width // SUB
    chunks = axial // LANES
    per_chunk = segments // chunks
    tile_rows = width // per_chunk
    total = rows * segments
    stiffness = radial_weight * rows * rows

    seg = lax.axis_index("rad")
    sec = lax.axis_index("azi")
    above = lax.rem(sec + 1, sectors)
    below = lax.rem(sec + sectors - 1, sectors)
    peers = [lax.rem(seg + k, segments) for k in range(1, segments)]
    first = seg * rows

    span = rows // 2
    loads = [
        [
            pltpu.make_async_copy(
                src.at[pl.ds(part_of * span, span)],
                dst.at[pl.ds(part_of * span, span)],
                in_sem.at[n, part_of],
            )
            for part_of in range(2)
        ]
        for n, (src, dst) in enumerate(
            (
                (start_hbm, state),
                (heat_hbm, heat),
                (size_hbm, size),
                (flux_hbm, flux),
                (goal_hbm, goal),
            )
        )
    ]
    for load in loads:
        for copy in load:
            copy.start()

    def await_load(load):
        for copy in load:
            copy.wait()

    barrier = pltpu.get_barrier_semaphore()
    for peer in peers:
        pl.semaphore_signal(barrier, inc=1, device_id=(peer, sec), device_id_type=MESH)
    for near in (above, below):
        pl.semaphore_signal(barrier, inc=1, device_id=(seg, near), device_id_type=MESH)

    def halo_copies(sweep):
        return [
            pltpu.make_async_remote_copy(
                src_ref=halo_out.at[sweep, side],
                dst_ref=halo_in.at[sweep, side],
                send_sem=halo_ssem.at[sweep, side],
                recv_sem=halo_rsem.at[sweep, side],
                device_id=(seg, near),
                device_id_type=MESH,
            )
            for side, near in ((0, above), (1, below))
        ]

    def sends(src, dst, ssem, rsem):
        return [
            pltpu.make_async_remote_copy(
                src_ref=src.at[peer],
                dst_ref=dst.at[seg],
                send_sem=ssem.at[peer],
                recv_sem=rsem.at[seg],
                device_id=(peer, sec),
                device_id_type=MESH,
            )
            for peer in peers
        ]

    def await_from(src, dst, ssem, rsem):
        for peer in peers:
            pltpu.make_async_remote_copy(
                src_ref=src.at[peer],
                dst_ref=dst.at[peer],
                send_sem=ssem.at[peer],
                recv_sem=rsem.at[peer],
                device_id=(peer, sec),
                device_id_type=MESH,
            ).wait_recv()

    def geometry(i):
        row = (first + i).astype(jnp.float32)
        radius = 1.0 + (row + 0.5) * (1.0 / total)
        low = stiffness * (1.0 + row * (1.0 / total))
        high = stiffness * (1.0 + (row + 1.0) * (1.0 / total))
        return radius, low, high

    def azimuth_coef(radius):
        return azimuth_weight / jnp.full((1, LANES), radius, jnp.float32)

    def wide(line):
        return jnp.concatenate([line] * chunks, axis=1)

    await_load(loads[0])

    def pack(i, carry):
        halo_out[0, 0, pl.ds(i, 1), :] = state[i, width - 1 : width, :]
        halo_out[0, 1, pl.ds(i, 1), :] = state[i, 0:1, :]
        return carry

    lax.fori_loop(0, rows, pack, 0, unroll=4)
    pl.semaphore_wait(barrier, segments + 1)
    halos = halo_copies(0)
    for copy in halos:
        copy.start()

    for load in loads[1:4]:
        await_load(load)

    def pieces():
        for c in range(chunks):
            for k in range(per_chunk):
                yield c * per_chunk + k, slice(k * tile_rows, (k + 1) * tile_rows), c

    def scatter(ref, slot, plane, c_first, c_last):
        for owner, where_rows, c in pieces():
            if c_first <= c < c_last:
                at = (c - c_first) * LANES
                ref[owner, slot] = plane[where_rows, at : at + LANES]

    half = 2 * LANES
    for h in range(axial // half):
        cols = slice(h * half, (h + 1) * half)

        def eliminate(i, carry):
            ratio, ea, prod, va, _ = carry
            radius, low, high = geometry(i)
            az2 = 2.0 * azimuth_coef(radius)
            az2 = jnp.concatenate([az2, az2], axis=1)
            viscosity = jnp.exp(
                arrhenius_exponent - arrhenius_exponent * heat[i, :, cols]
            )
            extent = size[i, :, cols]
            shear = (heat_weight * arrhenius_exponent) * viscosity * extent
            ahead = radius * (axial_weight + flow_weight * flux[i, :, cols])
            excess = (
                ahead + radius * (shear * extent + (mass_weight + axial_weight)) + az2
            )
            top = low * ratio + excess
            inverse = 1.0 / (top + high)
            ratio = top * inverse
            ea = (low * inverse) * ea
            upper = high * inverse
            va = va + prod * ea
            prod = prod * upper
            flux[i, :, cols] = ahead
            size[i, :, cols] = shear
            inv[i, :, cols] = inverse
            qa[i, :, cols] = ea
            return ratio, ea, prod, va, upper

        one = jnp.ones((width, half), jnp.float32)
        zero = jnp.zeros((width, half), jnp.float32)
        _, ea, _, va, upper = lax.fori_loop(
            0, rows, eliminate, (one, one, one, zero, zero)
        )
        scatter(coef_out, 0, va, 2 * h, 2 * h + 2)
        scatter(coef_out, 1, ea, 2 * h, 2 * h + 2)
        scatter(coef_out, 2, upper, 2 * h, 2 * h + 2)

    coef_sends = sends(coef_out, coef_in, coef_ssem, coef_rsem)
    for copy in coef_sends:
        copy.start()
    coef_in[seg] = coef_out[seg]

    def respond(n, carry):
        q_next, r_next = carry
        i = rows - 1 - n
        _, _, high = geometry(i)
        upper = high * inv[i]
        q_next = qa[i] + upper * q_next
        r_next = upper * r_next
        qa[i] = q_next
        rb[i] = r_next
        return q_next, r_next

    lax.fori_loop(
        0,
        rows,
        respond,
        (jnp.zeros((width, axial), jnp.float32), jnp.ones((width, axial), jnp.float32)),
    )

    await_load(loads[4])
    sub = lax.broadcasted_iota(jnp.int32, (SUB, axial), 0)
    lane = lax.broadcasted_iota(jnp.int32, (SUB, axial), 1)

    def right_side(sweep, chosen):
        def step(i, carry):
            radius, _, _ = geometry(i)
            az = wide(azimuth_coef(radius))
            rolled_up, rolled_down, new = {}, {}, []

            def block(g):
                return state[i, g * SUB : (g + 1) * SUB, :]

            def up(g):
                if g < 0:
                    return jnp.broadcast_to(
                        halo_in[sweep, 0, pl.ds(i, 1), :], (SUB, axial)
                    )
                if g not in rolled_up:
                    rolled_up[g] = pltpu.roll(block(g), 1, 0)
                return rolled_up[g]

            def down(g):
                if g >= groups:
                    return jnp.broadcast_to(
                        halo_in[sweep, 1, pl.ds(i, 1), :], (SUB, axial)
                    )
                if g not in rolled_down:
                    rolled_down[g] = pltpu.roll(block(g), SUB - 1, 0)
                return rolled_down[g]

            for g, (u_first, u_last) in zip(chosen, carry):
                here = slice(g * SUB, (g + 1) * SUB)
                x = block(g)
                sides = jnp.where(sub == 0, up(g - 1), up(g)) + jnp.where(
                    sub == SUB - 1, down(g + 1), down(g)
                )
                before = jnp.where(lane == 0, 0.0, pltpu.roll(x, 1, 1))
                after = jnp.where(lane == axial - 1, 0.0, pltpu.roll(x, axial - 1, 1))
                value = (
                    radius * (goal[i, here, :] + mass_weight * x + axial_weight * before)
                    + flux[i, here, :] * after
                    + az * sides
                )
                rhs[i, here, :] = value
                new.append(
                    (u_first + qa[i, here, :] * value, u_last + rb[i, here, :] * value)
                )
            return tuple(new)

        zero = jnp.zeros((SUB, axial), jnp.float32)
        sums = lax.fori_loop(0, rows, step, tuple((zero, zero) for _ in chosen))
        for g, pair in zip(chosen, sums):
            for slot, plane in enumerate(pair):
                for owner, where_rows, c in pieces():
                    at = g * SUB - where_rows.start
                    if 0 <= at < tile_rows:
                        u_out[sweep, owner, slot, at : at + SUB, :] = plane[
                            :, c * LANES : (c + 1) * LANES
                        ]

    def send_ends(sweep):
        copies = sends(
            u_out.at[sweep], u_in.at[sweep], u_ssem.at[sweep], u_rsem.at[sweep]
        )
        for copy in copies:
            copy.start()
        u_in[sweep, seg] = u_out[sweep, seg]
        return copies

    def await_ends(sweep):
        await_from(u_out.at[sweep], u_in.at[sweep], u_ssem.at[sweep], u_rsem.at[sweep])

    def substitute():
        def forward(i, g):
            _, low, _ = geometry(i)
            g = inv[i] * (rhs[i] + low * g)
            rhs[i] = g
            return g

        def backward(n, p):
            i = rows - 1 - n
            _, _, high = geometry(i)
            p = rhs[i] + (high * inv[i]) * p
            part[i] = p
            return p

        zero = jnp.zeros((width, axial), jnp.float32)
        lax.fori_loop(0, rows, forward, zero)
        lax.fori_loop(0, rows, backward, zero)

    def reduced_factors():
        factors, beta = [], None
        for s in range(segments):
            v_first, v_last, w_last = coef_in[s, 0], coef_in[s, 1], coef_in[s, 2]
            w_first = v_last * ((segments + s + 1.0) / (segments + s))
            if s == 0:
                factors.append((None, None, None, w_first, w_last, None))
                beta = w_last
                continue
            scale = 1.0 / (1.0 - v_first * beta)
            q = scale * w_first
            cross = v_last * beta
            new_beta = w_last + cross * q
            factors.append((scale, scale * v_first, v_last, q, new_beta, cross))
            beta = new_beta
        return factors

    def reduced_solve(sweep, factors):
        firsts, lasts = [], []
        for s in range(segments):
            u_first = u_in[sweep, s, 0] * (segments / (stiffness * (segments + s)))
            u_last = u_in[sweep, s, 1] * (segments / (stiffness * (segments + s + 1)))
            if s == 0:
                firsts.append(u_first)
                lasts.append(u_last)
                continue
            scale, scaled_v, v_last, _, _, cross = factors[s]
            p = scale * u_first + scaled_v * lasts[s - 1]
            firsts.append(p)
            lasts.append(u_last + v_last * lasts[s - 1] + cross * p)
        blank = jnp.zeros((tile_rows, LANES), jnp.float32)
        beyond = blank
        ret_out[sweep, 0, 0] = blank
        for s in range(segments - 1, -1, -1):
            ret_out[sweep, s, 1] = beyond
            if s < segments - 1:
                ret_out[sweep, s + 1, 0] = lasts[s] + factors[s][4] * beyond
            beyond = firsts[s] + factors[s][3] * beyond if s > 0 else beyond

    def send_back(sweep):
        copies = sends(
            ret_out.at[sweep], ret_in.at[sweep], ret_ssem.at[sweep], ret_rsem.at[sweep]
        )
        for copy in copies:
            copy.start()
        ret_in[sweep, seg] = ret_out[sweep, seg]
        return copies

    def await_back(sweep):
        await_from(
            ret_out.at[sweep], ret_in.at[sweep], ret_ssem.at[sweep], ret_rsem.at[sweep]
        )

    def ends(sweep):
        planes = []
        for slot in range(2):
            planes.append(
                jnp.concatenate(
                    [
                        jnp.concatenate(
                            [
                                ret_in[sweep, c * per_chunk + k, slot]
                                for k in range(per_chunk)
                            ],
                            axis=0,
                        )
                        for c in range(chunks)
                    ],
                    axis=1,
                )
            )
        return planes

    for copy in halos:
        copy.wait_recv()
    right_side(0, tuple(range(groups)))
    started = [coef_sends, halos, send_ends(0)]
    substitute()
    await_from(coef_out, coef_in, coef_ssem, coef_rsem)
    factors = reduced_factors()
    await_ends(0)
    reduced_solve(0, factors)
    started.append(send_back(0))

    last_lane = lax.broadcasted_iota(jnp.int32, (width, axial), 1) == axial - 1

    def slope(i, carry):
        here = heat[i]
        rise = jnp.where(last_lane, 0.0, pltpu.roll(here, axial - 1, 1) - here)
        heat[i] = slope_weight * rise - size[i]
        return carry

    lax.fori_loop(0, rows, slope, 0)

    await_back(0)
    a, b = ends(0)

    def advance(i, carry):
        x = part[i] + qa[i] * a + rb[i] * b
        state[i] = x
        halo_out[1, 0, pl.ds(i, 1), :] = x[width - 1 : width, :]
        halo_out[1, 1, pl.ds(i, 1), :] = x[0:1, :]
        return carry

    lax.fori_loop(0, rows, advance, 0)
    halos = halo_copies(1)
    for copy in halos:
        copy.start()

    for copy in halos:
        copy.wait_recv()
    right_side(1, tuple(range(groups)))
    started += [halos, send_ends(1)]
    substitute()
    await_ends(1)
    reduced_solve(1, reduced_factors())
    started.append(send_back(1))
    await_back(1)
    a, b = ends(1)

    quarter = rows // 4
    stores = []
    for n in range(4):

        def finish(i, carry):
            x = part[i] + qa[i] * a + rb[i] * b
            out_x[i] = x
            out_s[i] = x * heat[i]
            return carry

        lax.fori_loop(n * quarter, (n + 1) * quarter, finish, 0)
        span = slice(n * quarter, (n + 1) * quarter)
        for m, (src, dst) in enumerate(((out_x, adjoint_hbm), (out_s, sens_hbm))):
            store = pltpu.make_async_copy(
                src.at[pl.ds(n * quarter, quarter)],
                dst.at[pl.ds(n * quarter, quarter)],
                out_sem.at[m, n],
            )
            store.start()
            stores.append(store)

    for copies in started:
        for copy in copies:
            copy.wait_send()
    for store in stores:
        store.wait()


def solution(mesh):
    segments, sectors = mesh.shape["rad"], mesh.shape["azi"]
    spec = P("rad", "azi", None)

    def body(heat, size, flux, goal, start):
        rows, width, axial = heat.shape
        tile_rows = width * axial // (segments * LANES)
        block = pltpu.VMEM((rows, width, axial), jnp.float32)
        tile = (tile_rows, LANES)
        shape = jax.ShapeDtypeStruct((rows, width, axial), jnp.float32)
        dma = pltpu.SemaphoreType.DMA
        cells = rows * width * axial
        return pl.pallas_call(
            functools.partial(kernel, segments, sectors),
            out_shape=(shape, shape),
            in_specs=[pl.BlockSpec(memory_space=pltpu.HBM)] * 5,
            out_specs=[pl.BlockSpec(memory_space=pl.ANY)] * 2,
            scratch_shapes=[block] * 12
            + [
                pltpu.VMEM((2, 2, rows, axial), jnp.float32),
                pltpu.VMEM((2, 2, rows, axial), jnp.float32),
                pltpu.VMEM((segments, 3) + tile, jnp.float32),
                pltpu.VMEM((segments, 3) + tile, jnp.float32),
                pltpu.VMEM((2, segments, 2) + tile, jnp.float32),
                pltpu.VMEM((2, segments, 2) + tile, jnp.float32),
                pltpu.VMEM((2, segments, 2) + tile, jnp.float32),
                pltpu.VMEM((2, segments, 2) + tile, jnp.float32),
                dma((5, 2)),
                dma((2, 4)),
                dma((2, 2)),
                dma((2, 2)),
                dma((segments,)),
                dma((segments,)),
                dma((2, segments)),
                dma((2, segments)),
                dma((2, segments)),
                dma((2, segments)),
            ],
            compiler_params=pltpu.CompilerParams(
                collective_id=0, has_side_effects=True, vmem_limit_bytes=60 * 2**20
            ),
            cost_estimate=pl.CostEstimate(
                flops=120 * cells, bytes_accessed=28 * cells, transcendentals=2 * cells
            ),
        )(heat, size, flux, goal, start)

    return jax.shard_map(
        body, mesh=mesh, in_specs=(spec,) * 5, out_specs=(spec, spec), check_vma=False
    )
```

```python
import functools

import jax
import jax.numpy as jnp
from jax import lax
from jax.experimental import pallas as pl
from jax.experimental.pallas import tpu as pltpu
from jax.sharding import PartitionSpec as P

radial_weight = 8.0
azimuth_weight = 0.25
axial_weight = 0.25
flow_weight = 0.5
mass_weight = 1.0
heat_weight = 0.25
arrhenius_exponent = 2.0
slope_weight = 2.0

MESH = pl.DeviceIdType.MESH
LANES = 128
SUB = 8


def kernel(
    segments,
    sectors,
    heat_hbm,
    size_hbm,
    flux_hbm,
    goal_hbm,
    start_hbm,
    adjoint_hbm,
    sens_hbm,
    heat,
    size,
    flux,
    goal,
    state,
    inv,
    qa,
    rb,
    rhs,
    part,
    out_x,
    out_s,
    halo_out,
    halo_in,
    coef_out,
    coef_in,
    u_out,
    u_in,
    ret_out,
    ret_in,
    in_sem,
    out_sem,
    halo_ssem,
    halo_rsem,
    coef_ssem,
    coef_rsem,
    u_ssem,
    u_rsem,
    ret_ssem,
    ret_rsem,
):
    rows, width, axial = heat.shape
    groups = width // SUB
    chunks = axial // LANES
    per_chunk = segments // chunks
    tile_rows = width // per_chunk
    total = rows * segments
    stiffness = radial_weight * rows * rows

    seg = lax.axis_index("rad")
    sec = lax.axis_index("azi")
    above = lax.rem(sec + 1, sectors)
    below = lax.rem(sec + sectors - 1, sectors)
    peers = [lax.rem(seg + k, segments) for k in range(1, segments)]
    first = seg * rows

    span = rows // 2
    loads = [
        [
            pltpu.make_async_copy(
                src.at[pl.ds(part_of * span, span)],
                dst.at[pl.ds(part_of * span, span)],
                in_sem.at[n, part_of],
            )
            for part_of in range(2)
        ]
        for n, (src, dst) in enumerate(
            (
                (start_hbm, state),
                (heat_hbm, heat),
                (size_hbm, size),
                (flux_hbm, flux),
                (goal_hbm, goal),
            )
        )
    ]
    for load in loads:
        for copy in load:
            copy.start()

    def await_load(load):
        for copy in load:
            copy.wait()

    barrier = pltpu.get_barrier_semaphore()
    for peer in peers:
        pl.semaphore_signal(barrier, inc=1, device_id=(peer, sec), device_id_type=MESH)
    for near in (above, below):
        pl.semaphore_signal(barrier, inc=1, device_id=(seg, near), device_id_type=MESH)

    def halo_copies(sweep):
        return [
            pltpu.make_async_remote_copy(
                src_ref=halo_out.at[sweep, side],
                dst_ref=halo_in.at[sweep, side],
                send_sem=halo_ssem.at[sweep, side],
                recv_sem=halo_rsem.at[sweep, side],
                device_id=(seg, near),
                device_id_type=MESH,
            )
            for side, near in ((0, above), (1, below))
        ]

    def sends(src, dst, ssem, rsem):
        return [
            pltpu.make_async_remote_copy(
                src_ref=src.at[peer],
                dst_ref=dst.at[seg],
                send_sem=ssem.at[peer],
                recv_sem=rsem.at[seg],
                device_id=(peer, sec),
                device_id_type=MESH,
            )
            for peer in peers
        ]

    def await_from(src, dst, ssem, rsem):
        for peer in peers:
            pltpu.make_async_remote_copy(
                src_ref=src.at[peer],
                dst_ref=dst.at[peer],
                send_sem=ssem.at[peer],
                recv_sem=rsem.at[peer],
                device_id=(peer, sec),
                device_id_type=MESH,
            ).wait_recv()

    def geometry(i):
        row = (first + i).astype(jnp.float32)
        radius = 1.0 + (row + 0.5) * (1.0 / total)
        low = stiffness * (1.0 + row * (1.0 / total))
        high = stiffness * (1.0 + (row + 1.0) * (1.0 / total))
        return radius, low, high

    def azimuth_coef(radius):
        return azimuth_weight / jnp.full((1, LANES), radius, jnp.float32)

    def wide(line):
        return jnp.concatenate([line] * chunks, axis=1)

    await_load(loads[0])

    def pack(i, carry):
        halo_out[0, 0, pl.ds(i, 1), :] = state[i, width - 1 : width, :]
        halo_out[0, 1, pl.ds(i, 1), :] = state[i, 0:1, :]
        return carry

    lax.fori_loop(0, rows, pack, 0, unroll=4)
    pl.semaphore_wait(barrier, segments + 1)
    halos = halo_copies(0)
    for copy in halos:
        copy.start()

    for load in loads[1:4]:
        await_load(load)

    def pieces():
        for c in range(chunks):
            for k in range(per_chunk):
                yield c * per_chunk + k, slice(k * tile_rows, (k + 1) * tile_rows), c

    def scatter(ref, slot, plane, c_first, c_last):
        for owner, where_rows, c in pieces():
            if c_first <= c < c_last:
                at = (c - c_first) * LANES
                ref[owner, slot] = plane[where_rows, at : at + LANES]

    half = 2 * LANES
    for h in range(axial // half):
        cols = slice(h * half, (h + 1) * half)

        def eliminate(i, carry):
            ratio, ea, prod, va, _ = carry
            radius, low, high = geometry(i)
            az2 = 2.0 * azimuth_coef(radius)
            az2 = jnp.concatenate([az2, az2], axis=1)
            viscosity = jnp.exp(
                arrhenius_exponent - arrhenius_exponent * heat[i, :, cols]
            )
            extent = size[i, :, cols]
            shear = (heat_weight * arrhenius_exponent) * viscosity * extent
            ahead = radius * (axial_weight + flow_weight * flux[i, :, cols])
            excess = (
                ahead + radius * (shear * extent + (mass_weight + axial_weight)) + az2
            )
            top = low * ratio + excess
            inverse = 1.0 / (top + high)
            ratio = top * inverse
            ea = (low * inverse) * ea
            upper = high * inverse
            va = va + prod * ea
            prod = prod * upper
            flux[i, :, cols] = ahead
            size[i, :, cols] = shear
            inv[i, :, cols] = inverse
            qa[i, :, cols] = ea
            return ratio, ea, prod, va, upper

        one = jnp.ones((width, half), jnp.float32)
        zero = jnp.zeros((width, half), jnp.float32)
        _, ea, _, va, upper = lax.fori_loop(
            0, rows, eliminate, (one, one, one, zero, zero), unroll=4
        )
        scatter(coef_out, 0, va, 2 * h, 2 * h + 2)
        scatter(coef_out, 1, ea, 2 * h, 2 * h + 2)
        scatter(coef_out, 2, upper, 2 * h, 2 * h + 2)

    coef_sends = sends(coef_out, coef_in, coef_ssem, coef_rsem)
    for copy in coef_sends:
        copy.start()
    coef_in[seg] = coef_out[seg]

    def respond(n, carry):
        q_next, r_next = carry
        i = rows - 1 - n
        _, _, high = geometry(i)
        upper = high * inv[i]
        q_next = qa[i] + upper * q_next
        r_next = upper * r_next
        qa[i] = q_next
        rb[i] = r_next
        return q_next, r_next

    lax.fori_loop(
        0,
        rows,
        respond,
        (jnp.zeros((width, axial), jnp.float32), jnp.ones((width, axial), jnp.float32)),
        unroll=4,
    )

    await_load(loads[4])
    sub = lax.broadcasted_iota(jnp.int32, (SUB, axial), 0)
    lane = lax.broadcasted_iota(jnp.int32, (SUB, axial), 1)

    def right_side(sweep, chosen):
        def step(i, carry):
            radius, _, _ = geometry(i)
            az = wide(azimuth_coef(radius))
            rolled_up, rolled_down, new = {}, {}, []

            def block(g):
                return state[i, g * SUB : (g + 1) * SUB, :]

            def up(g):
                if g < 0:
                    return jnp.broadcast_to(
                        halo_in[sweep, 0, pl.ds(i, 1), :], (SUB, axial)
                    )
                if g not in rolled_up:
                    rolled_up[g] = pltpu.roll(block(g), 1, 0)
                return rolled_up[g]

            def down(g):
                if g >= groups:
                    return jnp.broadcast_to(
                        halo_in[sweep, 1, pl.ds(i, 1), :], (SUB, axial)
                    )
                if g not in rolled_down:
                    rolled_down[g] = pltpu.roll(block(g), SUB - 1, 0)
                return rolled_down[g]

            for g, (u_first, u_last) in zip(chosen, carry):
                here = slice(g * SUB, (g + 1) * SUB)
                x = block(g)
                sides = jnp.where(sub == 0, up(g - 1), up(g)) + jnp.where(
                    sub == SUB - 1, down(g + 1), down(g)
                )
                before = jnp.where(lane == 0, 0.0, pltpu.roll(x, 1, 1))
                after = jnp.where(lane == axial - 1, 0.0, pltpu.roll(x, axial - 1, 1))
                value = (
                    radius * (goal[i, here, :] + mass_weight * x + axial_weight * before)
                    + flux[i, here, :] * after
                    + az * sides
                )
                rhs[i, here, :] = value
                new.append(
                    (u_first + qa[i, here, :] * value, u_last + rb[i, here, :] * value)
                )
            return tuple(new)

        zero = jnp.zeros((SUB, axial), jnp.float32)
        sums = lax.fori_loop(0, rows, step, tuple((zero, zero) for _ in chosen), unroll=2)
        for g, pair in zip(chosen, sums):
            for slot, plane in enumerate(pair):
                for owner, where_rows, c in pieces():
                    at = g * SUB - where_rows.start
                    if 0 <= at < tile_rows:
                        u_out[sweep, owner, slot, at : at + SUB, :] = plane[
                            :, c * LANES : (c + 1) * LANES
                        ]

    def send_ends(sweep):
        copies = sends(
            u_out.at[sweep], u_in.at[sweep], u_ssem.at[sweep], u_rsem.at[sweep]
        )
        for copy in copies:
            copy.start()
        u_in[sweep, seg] = u_out[sweep, seg]
        return copies

    def await_ends(sweep):
        await_from(u_out.at[sweep], u_in.at[sweep], u_ssem.at[sweep], u_rsem.at[sweep])

    def substitute():
        def forward(i, g):
            _, low, _ = geometry(i)
            g = inv[i] * (rhs[i] + low * g)
            rhs[i] = g
            return g

        def backward(n, p):
            i = rows - 1 - n
            _, _, high = geometry(i)
            p = rhs[i] + (high * inv[i]) * p
            part[i] = p
            return p

        zero = jnp.zeros((width, axial), jnp.float32)
        lax.fori_loop(0, rows, forward, zero, unroll=4)
        lax.fori_loop(0, rows, backward, zero, unroll=4)

    def reduced_factors():
        factors, beta = [], None
        for s in range(segments):
            v_first, v_last, w_last = coef_in[s, 0], coef_in[s, 1], coef_in[s, 2]
            w_first = v_last * ((segments + s + 1.0) / (segments + s))
            if s == 0:
                factors.append((None, None, None, w_first, w_last, None))
                beta = w_last
                continue
            scale = 1.0 / (1.0 - v_first * beta)
            q = scale * w_first
            cross = v_last * beta
            new_beta = w_last + cross * q
            factors.append((scale, scale * v_first, v_last, q, new_beta, cross))
            beta = new_beta
        return factors

    def reduced_solve(sweep, factors):
        firsts, lasts = [], []
        for s in range(segments):
            u_first = u_in[sweep, s, 0] * (segments / (stiffness * (segments + s)))
            u_last = u_in[sweep, s, 1] * (segments / (stiffness * (segments + s + 1)))
            if s == 0:
                firsts.append(u_first)
                lasts.append(u_last)
                continue
            scale, scaled_v, v_last, _, _, cross = factors[s]
            p = scale * u_first + scaled_v * lasts[s - 1]
            firsts.append(p)
            lasts.append(u_last + v_last * lasts[s - 1] + cross * p)
        blank = jnp.zeros((tile_rows, LANES), jnp.float32)
        beyond = blank
        ret_out[sweep, 0, 0] = blank
        for s in range(segments - 1, -1, -1):
            ret_out[sweep, s, 1] = beyond
            if s < segments - 1:
                ret_out[sweep, s + 1, 0] = lasts[s] + factors[s][4] * beyond
            beyond = firsts[s] + factors[s][3] * beyond if s > 0 else beyond

    def send_back(sweep):
        copies = sends(
            ret_out.at[sweep], ret_in.at[sweep], ret_ssem.at[sweep], ret_rsem.at[sweep]
        )
        for copy in copies:
            copy.start()
        ret_in[sweep, seg] = ret_out[sweep, seg]
        return copies

    def await_back(sweep):
        await_from(
            ret_out.at[sweep], ret_in.at[sweep], ret_ssem.at[sweep], ret_rsem.at[sweep]
        )

    def ends(sweep):
        planes = []
        for slot in range(2):
            planes.append(
                jnp.concatenate(
                    [
                        jnp.concatenate(
                            [
                                ret_in[sweep, c * per_chunk + k, slot]
                                for k in range(per_chunk)
                            ],
                            axis=0,
                        )
                        for c in range(chunks)
                    ],
                    axis=1,
                )
            )
        return planes

    for copy in halos:
        copy.wait_recv()
    right_side(0, tuple(range(groups)))
    started = [coef_sends, halos, send_ends(0)]
    substitute()
    await_from(coef_out, coef_in, coef_ssem, coef_rsem)
    factors = reduced_factors()
    await_ends(0)
    reduced_solve(0, factors)
    started.append(send_back(0))

    last_lane = lax.broadcasted_iota(jnp.int32, (width, axial), 1) == axial - 1

    def slope(i, carry):
        here = heat[i]
        rise = jnp.where(last_lane, 0.0, pltpu.roll(here, axial - 1, 1) - here)
        heat[i] = slope_weight * rise - size[i]
        return carry

    lax.fori_loop(0, rows, slope, 0, unroll=4)

    await_back(0)
    a, b = ends(0)

    def advance(i, carry):
        x = part[i] + qa[i] * a + rb[i] * b
        state[i] = x
        halo_out[1, 0, pl.ds(i, 1), :] = x[width - 1 : width, :]
        halo_out[1, 1, pl.ds(i, 1), :] = x[0:1, :]
        return carry

    lax.fori_loop(0, rows, advance, 0, unroll=4)
    halos = halo_copies(1)
    for copy in halos:
        copy.start()

    for copy in halos:
        copy.wait_recv()
    right_side(1, tuple(range(groups)))
    started += [halos, send_ends(1)]
    substitute()
    await_ends(1)
    reduced_solve(1, reduced_factors())
    started.append(send_back(1))
    await_back(1)
    a, b = ends(1)

    quarter = rows // 4
    stores = []
    for n in range(4):

        def finish(i, carry):
            x = part[i] + qa[i] * a + rb[i] * b
            out_x[i] = x
            out_s[i] = x * heat[i]
            return carry

        lax.fori_loop(n * quarter, (n + 1) * quarter, finish, 0, unroll=4)
        span = slice(n * quarter, (n + 1) * quarter)
        for m, (src, dst) in enumerate(((out_x, adjoint_hbm), (out_s, sens_hbm))):
            store = pltpu.make_async_copy(
                src.at[pl.ds(n * quarter, quarter)],
                dst.at[pl.ds(n * quarter, quarter)],
                out_sem.at[m, n],
            )
            store.start()
            stores.append(store)

    for copies in started:
        for copy in copies:
            copy.wait_send()
    for store in stores:
        store.wait()


def solution(mesh):
    segments, sectors = mesh.shape["rad"], mesh.shape["azi"]
    spec = P("rad", "azi", None)

    def body(heat, size, flux, goal, start):
        rows, width, axial = heat.shape
        tile_rows = width * axial // (segments * LANES)
        block = pltpu.VMEM((rows, width, axial), jnp.float32)
        tile = (tile_rows, LANES)
        shape = jax.ShapeDtypeStruct((rows, width, axial), jnp.float32)
        dma = pltpu.SemaphoreType.DMA
        cells = rows * width * axial
        return pl.pallas_call(
            functools.partial(kernel, segments, sectors),
            out_shape=(shape, shape),
            in_specs=[pl.BlockSpec(memory_space=pltpu.HBM)] * 5,
            out_specs=[pl.BlockSpec(memory_space=pl.ANY)] * 2,
            scratch_shapes=[block] * 12
            + [
                pltpu.VMEM((2, 2, rows, axial), jnp.float32),
                pltpu.VMEM((2, 2, rows, axial), jnp.float32),
                pltpu.VMEM((segments, 3) + tile, jnp.float32),
                pltpu.VMEM((segments, 3) + tile, jnp.float32),
                pltpu.VMEM((2, segments, 2) + tile, jnp.float32),
                pltpu.VMEM((2, segments, 2) + tile, jnp.float32),
                pltpu.VMEM((2, segments, 2) + tile, jnp.float32),
                pltpu.VMEM((2, segments, 2) + tile, jnp.float32),
                dma((5, 2)),
                dma((2, 4)),
                dma((2, 2)),
                dma((2, 2)),
                dma((segments,)),
                dma((segments,)),
                dma((2, segments)),
                dma((2, segments)),
                dma((2, segments)),
                dma((2, segments)),
            ],
            compiler_params=pltpu.CompilerParams(
                collective_id=0, has_side_effects=True, vmem_limit_bytes=60 * 2**20
            ),
            cost_estimate=pl.CostEstimate(
                flops=120 * cells, bytes_accessed=28 * cells, transcendentals=2 * cells
            ),
        )(heat, size, flux, goal, start)

    return jax.shard_map(
        body, mesh=mesh, in_specs=(spec,) * 5, out_specs=(spec, spec), check_vma=False
    )
```

```python
import functools

import jax
import jax.numpy as jnp
from jax import lax
from jax.experimental import pallas as pl
from jax.experimental.pallas import tpu as pltpu
from jax.sharding import PartitionSpec as P

radial_weight = 8.0
azimuth_weight = 0.25
axial_weight = 0.25
flow_weight = 0.5
mass_weight = 1.0
heat_weight = 0.25
arrhenius_exponent = 2.0
slope_weight = 2.0

MESH = pl.DeviceIdType.MESH
LANES = 128
SUB = 8


def kernel(
    segments,
    sectors,
    heat_hbm,
    size_hbm,
    flux_hbm,
    goal_hbm,
    start_hbm,
    adjoint_hbm,
    sens_hbm,
    heat,
    size,
    flux,
    goal,
    state,
    inv,
    qa,
    rb,
    rhs,
    part,
    out_x,
    out_s,
    halo_out,
    halo_in,
    coef_out,
    coef_in,
    u_out,
    u_in,
    ret_out,
    ret_in,
    factor,
    side_a,
    side_b,
    in_sem,
    out_sem,
    halo_ssem,
    halo_rsem,
    coef_ssem,
    coef_rsem,
    u_ssem,
    u_rsem,
    ret_ssem,
    ret_rsem,
):
    rows, width, axial = heat.shape
    groups = width // SUB
    chunks = axial // LANES
    per_chunk = segments // chunks
    tile_rows = width // (2 * per_chunk)
    inner, outer = tuple(range(1, groups - 1)), (0, groups - 1)
    halves = (inner, outer)
    total = rows * segments
    stiffness = radial_weight * rows * rows

    seg = lax.axis_index("rad")
    sec = lax.axis_index("azi")
    above = lax.rem(sec + 1, sectors)
    below = lax.rem(sec + sectors - 1, sectors)
    peers = [lax.rem(seg + k, segments) for k in range(1, segments)]
    first = seg * rows

    span = rows // 2
    loads = [
        [
            pltpu.make_async_copy(
                src.at[pl.ds(part_of * span, span)],
                dst.at[pl.ds(part_of * span, span)],
                in_sem.at[n, part_of],
            )
            for part_of in range(2)
        ]
        for n, (src, dst) in enumerate(
            (
                (start_hbm, state),
                (heat_hbm, heat),
                (size_hbm, size),
                (flux_hbm, flux),
                (goal_hbm, goal),
            )
        )
    ]
    for load in loads:
        for copy in load:
            copy.start()

    def await_load(load):
        for copy in load:
            copy.wait()

    barrier = pltpu.get_barrier_semaphore()
    for peer in peers:
        pl.semaphore_signal(barrier, inc=1, device_id=(peer, sec), device_id_type=MESH)
    for near in (above, below):
        pl.semaphore_signal(barrier, inc=1, device_id=(seg, near), device_id_type=MESH)

    def halo_copies(sweep):
        return [
            pltpu.make_async_remote_copy(
                src_ref=halo_out.at[sweep, side],
                dst_ref=halo_in.at[sweep, side],
                send_sem=halo_ssem.at[sweep, side],
                recv_sem=halo_rsem.at[sweep, side],
                device_id=(seg, near),
                device_id_type=MESH,
            )
            for side, near in ((0, above), (1, below))
        ]

    def sends(src, dst, ssem, rsem):
        return [
            pltpu.make_async_remote_copy(
                src_ref=src.at[peer],
                dst_ref=dst.at[seg],
                send_sem=ssem.at[peer],
                recv_sem=rsem.at[seg],
                device_id=(peer, sec),
                device_id_type=MESH,
            )
            for peer in peers
        ]

    def await_from(src, dst, ssem, rsem):
        for peer in peers:
            pltpu.make_async_remote_copy(
                src_ref=src.at[peer],
                dst_ref=dst.at[peer],
                send_sem=ssem.at[peer],
                recv_sem=rsem.at[peer],
                device_id=(peer, sec),
                device_id_type=MESH,
            ).wait_recv()

    def geometry(i):
        row = (first + i).astype(jnp.float32)
        radius = 1.0 + (row + 0.5) * (1.0 / total)
        low = stiffness * (1.0 + row * (1.0 / total))
        high = stiffness * (1.0 + (row + 1.0) * (1.0 / total))
        return radius, low, high

    def azimuth_coef(radius):
        return azimuth_weight / jnp.full((1, LANES), radius, jnp.float32)

    def wide(line):
        return jnp.concatenate([line] * chunks, axis=1)

    await_load(loads[0])

    def pack(i, carry):
        halo_out[0, 0, pl.ds(i, 1), :] = state[i, width - 1 : width, :]
        halo_out[0, 1, pl.ds(i, 1), :] = state[i, 0:1, :]
        return carry

    lax.fori_loop(0, rows, pack, 0, unroll=4)
    pl.semaphore_wait(barrier, segments + 1)
    halos = halo_copies(0)
    for copy in halos:
        copy.start()

    for load in loads[1:4]:
        await_load(load)

    def rows_of(g):
        return slice(g * SUB, (g + 1) * SUB)

    def pieces():
        for c in range(chunks):
            for k in range(per_chunk):
                where_rows = slice(k * tile_rows, (k + 1) * tile_rows)
                where_cols = slice(c * LANES, (c + 1) * LANES)
                yield c * per_chunk + k, where_rows, where_cols

    def scatter(slot, plane, c_first, c_last):
        for n, chosen in enumerate(halves):
            lines = jnp.concatenate([plane[rows_of(g)] for g in chosen], axis=0)
            for owner, where_rows, cols in pieces():
                if c_first * LANES <= cols.start < c_last * LANES:
                    at = cols.start - c_first * LANES
                    coef_out[owner, slot, n] = lines[where_rows, at : at + LANES]

    half = 2 * LANES
    for h in range(axial // half):
        cols = slice(h * half, (h + 1) * half)

        def eliminate(i, carry):
            ratio, ea, prod, va, _ = carry
            radius, low, high = geometry(i)
            az2 = 2.0 * azimuth_coef(radius)
            az2 = jnp.concatenate([az2, az2], axis=1)
            viscosity = jnp.exp(
                arrhenius_exponent - arrhenius_exponent * heat[i, :, cols]
            )
            extent = size[i, :, cols]
            shear = (heat_weight * arrhenius_exponent) * viscosity * extent
            ahead = radius * (axial_weight + flow_weight * flux[i, :, cols])
            excess = (
                ahead + radius * (shear * extent + (mass_weight + axial_weight)) + az2
            )
            top = low * ratio + excess
            inverse = 1.0 / (top + high)
            ratio = top * inverse
            ea = (low * inverse) * ea
            upper = high * inverse
            va = va + prod * ea
            prod = prod * upper
            flux[i, :, cols] = ahead
            size[i, :, cols] = shear
            inv[i, :, cols] = inverse
            qa[i, :, cols] = ea
            return ratio, ea, prod, va, upper

        one = jnp.ones((width, half), jnp.float32)
        zero = jnp.zeros((width, half), jnp.float32)
        _, ea, _, va, upper = lax.fori_loop(
            0, rows, eliminate, (one, one, one, zero, zero), unroll=4
        )
        scatter(0, va, 2 * h, 2 * h + 2)
        scatter(1, ea, 2 * h, 2 * h + 2)
        scatter(2, upper, 2 * h, 2 * h + 2)

    coef_sends = sends(coef_out, coef_in, coef_ssem, coef_rsem)
    for copy in coef_sends:
        copy.start()
    coef_in[seg] = coef_out[seg]

    def respond(n, carry):
        q_next, r_next = carry
        i = rows - 1 - n
        _, _, high = geometry(i)
        upper = high * inv[i]
        q_next = qa[i] + upper * q_next
        r_next = upper * r_next
        qa[i] = q_next
        rb[i] = r_next
        return q_next, r_next

    lax.fori_loop(
        0,
        rows,
        respond,
        (jnp.zeros((width, axial), jnp.float32), jnp.ones((width, axial), jnp.float32)),
        unroll=4,
    )

    await_load(loads[4])
    sub = lax.broadcasted_iota(jnp.int32, (SUB, axial), 0)
    lane = lax.broadcasted_iota(jnp.int32, (SUB, axial), 1)

    def right_side(sweep, half):
        chosen = halves[half]

        def step(i, carry):
            radius, _, _ = geometry(i)
            az = wide(azimuth_coef(radius))
            rolled_up, rolled_down, new = {}, {}, []

            def block(g):
                return state[i, g * SUB : (g + 1) * SUB, :]

            def up(g):
                if g < 0:
                    return jnp.broadcast_to(
                        halo_in[sweep, 0, pl.ds(i, 1), :], (SUB, axial)
                    )
                if g not in rolled_up:
                    rolled_up[g] = pltpu.roll(block(g), 1, 0)
                return rolled_up[g]

            def down(g):
                if g >= groups:
                    return jnp.broadcast_to(
                        halo_in[sweep, 1, pl.ds(i, 1), :], (SUB, axial)
                    )
                if g not in rolled_down:
                    rolled_down[g] = pltpu.roll(block(g), SUB - 1, 0)
                return rolled_down[g]

            for g, (u_first, u_last) in zip(chosen, carry):
                here = slice(g * SUB, (g + 1) * SUB)
                x = block(g)
                sides = jnp.where(sub == 0, up(g - 1), up(g)) + jnp.where(
                    sub == SUB - 1, down(g + 1), down(g)
                )
                before = jnp.where(lane == 0, 0.0, pltpu.roll(x, 1, 1))
                after = jnp.where(lane == axial - 1, 0.0, pltpu.roll(x, axial - 1, 1))
                value = (
                    radius * (goal[i, here, :] + mass_weight * x + axial_weight * before)
                    + flux[i, here, :] * after
                    + az * sides
                )
                rhs[i, here, :] = value
                new.append(
                    (u_first + qa[i, here, :] * value, u_last + rb[i, here, :] * value)
                )
            return tuple(new)

        zero = jnp.zeros((SUB, axial), jnp.float32)
        sums = lax.fori_loop(0, rows, step, tuple((zero, zero) for _ in chosen), unroll=2)
        for slot in range(2):
            lines = jnp.concatenate([pair[slot] for pair in sums], axis=0)
            for owner, where_rows, cols in pieces():
                u_out[sweep, half, owner, slot] = lines[where_rows, cols]

    def send_ends(sweep, half):
        at = (sweep, half)
        copies = sends(u_out.at[at], u_in.at[at], u_ssem.at[at], u_rsem.at[at])
        for copy in copies:
            copy.start()
        u_in[sweep, half, seg] = u_out[sweep, half, seg]
        return copies

    def await_ends(sweep, half):
        at = (sweep, half)
        await_from(u_out.at[at], u_in.at[at], u_ssem.at[at], u_rsem.at[at])

    def substitute(half):
        chosen = halves[half]

        def forward(i, carry):
            _, low, _ = geometry(i)
            new = []
            for g, before in zip(chosen, carry):
                here = rows_of(g)
                now = inv[i, here, :] * (rhs[i, here, :] + low * before)
                rhs[i, here, :] = now
                new.append(now)
            return tuple(new)

        def backward(n, carry):
            i = rows - 1 - n
            _, _, high = geometry(i)
            new = []
            for g, after in zip(chosen, carry):
                here = rows_of(g)
                now = rhs[i, here, :] + (high * inv[i, here, :]) * after
                part[i, here, :] = now
                new.append(now)
            return tuple(new)

        zero = tuple(jnp.zeros((SUB, axial), jnp.float32) for _ in chosen)
        lax.fori_loop(0, rows, forward, zero, unroll=4)
        lax.fori_loop(0, rows, backward, zero, unroll=4)

    def reduced_factors(half):
        beta = None
        for s in range(segments):
            v_first, v_last, w_last = [coef_in[s, slot, half] for slot in range(3)]
            w_first = v_last * ((segments + s + 1.0) / (segments + s))
            if s == 0:
                beta = w_last
                factor[half, s, 3] = beta
                continue
            scale = 1.0 / (1.0 - v_first * beta)
            q = scale * w_first
            cross = v_last * beta
            beta = w_last + cross * q
            for slot, plane in enumerate((scale, scale * v_first, q, beta, cross)):
                factor[half, s, slot] = plane

    def reduced_solve(sweep, half):
        firsts, lasts = [], []
        for s in range(segments):
            end = [u_in[sweep, half, s, slot] for slot in range(2)]
            u_first = end[0] * (segments / (stiffness * (segments + s)))
            u_last = end[1] * (segments / (stiffness * (segments + s + 1)))
            if s == 0:
                firsts.append(u_first)
                lasts.append(u_last)
                continue
            p = factor[half, s, 0] * u_first + factor[half, s, 1] * lasts[s - 1]
            firsts.append(p)
            lasts.append(
                u_last + coef_in[s, 1, half] * lasts[s - 1] + factor[half, s, 4] * p
            )
        beyond = jnp.zeros((tile_rows, LANES), jnp.float32)
        ret_out[sweep, half, 0, 0] = beyond
        for s in range(segments - 1, -1, -1):
            ret_out[sweep, half, s, 1] = beyond
            if s < segments - 1:
                ret_out[sweep, half, s + 1, 0] = lasts[s] + factor[half, s, 3] * beyond
            if s > 0:
                beyond = firsts[s] + factor[half, s, 2] * beyond

    def send_back(sweep, half):
        at = (sweep, half)
        copies = sends(ret_out.at[at], ret_in.at[at], ret_ssem.at[at], ret_rsem.at[at])
        for copy in copies:
            copy.start()
        ret_in[sweep, half, seg] = ret_out[sweep, half, seg]
        return copies

    def ends(sweep, half):
        at = (sweep, half)
        await_from(ret_out.at[at], ret_in.at[at], ret_ssem.at[at], ret_rsem.at[at])
        for owner, where_rows, cols in pieces():
            side_a[half, where_rows, cols] = ret_in[sweep, half, owner, 0]
            side_b[half, where_rows, cols] = ret_in[sweep, half, owner, 1]
        return [
            (side_a[half, rows_of(n), :], side_b[half, rows_of(n), :])
            for n in range(len(halves[half]))
        ]

    def solved(i, half, sides):
        for g, (a, b) in zip(halves[half], sides):
            here = rows_of(g)
            yield g, part[i, here, :] + qa[i, here, :] * a + rb[i, here, :] * b

    for copy in halos:
        copy.wait_recv()
    started = [coef_sends, halos]
    for half in (1, 0):
        right_side(0, half)
        started.append(send_ends(0, half))
    await_from(coef_out, coef_in, coef_ssem, coef_rsem)
    for half in (1, 0):
        reduced_factors(half)
    for half in (1, 0):
        substitute(half)
        await_ends(0, half)
        reduced_solve(0, half)
        started.append(send_back(0, half))

    last_lane = lax.broadcasted_iota(jnp.int32, (width, axial), 1) == axial - 1

    def slope(i, carry):
        here = heat[i]
        rise = jnp.where(last_lane, 0.0, pltpu.roll(here, axial - 1, 1) - here)
        heat[i] = slope_weight * rise - size[i]
        return carry

    lax.fori_loop(0, rows, slope, 0, unroll=4)

    for half in (1, 0):
        sides = ends(0, half)

        def advance(i, carry):
            for g, x in solved(i, half, sides):
                state[i, rows_of(g), :] = x
                if g == groups - 1:
                    halo_out[1, 0, pl.ds(i, 1), :] = x[SUB - 1 : SUB, :]
                if g == 0:
                    halo_out[1, 1, pl.ds(i, 1), :] = x[0:1, :]
            return carry

        lax.fori_loop(0, rows, advance, 0, unroll=4)
        if half == 1:
            halos = halo_copies(1)
            started.append(halos)
            for copy in halos:
                copy.start()

    for half in (0, 1):
        if half == 1:
            for copy in halos:
                copy.wait_recv()
        right_side(1, half)
        started.append(send_ends(1, half))
    for half in (0, 1):
        substitute(half)
        await_ends(1, half)
        reduced_solve(1, half)
        started.append(send_back(1, half))

    stores = []
    for half in (0, 1):
        sides = ends(1, half)

        def finish(i, carry):
            for g, x in solved(i, half, sides):
                here = rows_of(g)
                out_x[i, here, :] = x
                out_s[i, here, :] = x * heat[i, here, :]
            return carry

        lax.fori_loop(0, rows, finish, 0, unroll=4)
        for g in halves[half]:
            here = pl.ds(g * SUB, SUB)
            for m, (src, dst) in enumerate(((out_x, adjoint_hbm), (out_s, sens_hbm))):
                store = pltpu.make_async_copy(
                    src.at[:, here], dst.at[:, here], out_sem.at[m, g]
                )
                store.start()
                stores.append(store)

    for copies in started:
        for copy in copies:
            copy.wait_send()
    for store in stores:
        store.wait()


def solution(mesh):
    segments, sectors = mesh.shape["rad"], mesh.shape["azi"]
    spec = P("rad", "azi", None)

    def body(heat, size, flux, goal, start):
        rows, width, axial = heat.shape
        half_rows = width // 2
        tile_rows = half_rows * axial // (segments * LANES)
        block = pltpu.VMEM((rows, width, axial), jnp.float32)
        tile = (tile_rows, LANES)
        shape = jax.ShapeDtypeStruct((rows, width, axial), jnp.float32)
        dma = pltpu.SemaphoreType.DMA
        cells = rows * width * axial
        return pl.pallas_call(
            functools.partial(kernel, segments, sectors),
            out_shape=(shape, shape),
            in_specs=[pl.BlockSpec(memory_space=pltpu.HBM)] * 5,
            out_specs=[pl.BlockSpec(memory_space=pl.ANY)] * 2,
            scratch_shapes=[block] * 12
            + [
                pltpu.VMEM((2, 2, rows, axial), jnp.float32),
                pltpu.VMEM((2, 2, rows, axial), jnp.float32),
                pltpu.VMEM((segments, 3, 2) + tile, jnp.float32),
                pltpu.VMEM((segments, 3, 2) + tile, jnp.float32),
                pltpu.VMEM((2, 2, segments, 2) + tile, jnp.float32),
                pltpu.VMEM((2, 2, segments, 2) + tile, jnp.float32),
                pltpu.VMEM((2, 2, segments, 2) + tile, jnp.float32),
                pltpu.VMEM((2, 2, segments, 2) + tile, jnp.float32),
                pltpu.VMEM((2, segments, 5) + tile, jnp.float32),
                pltpu.VMEM((2, half_rows, axial), jnp.float32),
                pltpu.VMEM((2, half_rows, axial), jnp.float32),
                dma((5, 2)),
                dma((2, width // SUB)),
                dma((2, 2)),
                dma((2, 2)),
                dma((segments,)),
                dma((segments,)),
                dma((2, 2, segments)),
                dma((2, 2, segments)),
                dma((2, 2, segments)),
                dma((2, 2, segments)),
            ],
            compiler_params=pltpu.CompilerParams(
                collective_id=0, has_side_effects=True, vmem_limit_bytes=60 * 2**20
            ),
            cost_estimate=pl.CostEstimate(
                flops=120 * cells, bytes_accessed=28 * cells, transcendentals=2 * cells
            ),
        )(heat, size, flux, goal, start)

    return jax.shard_map(
        body, mesh=mesh, in_specs=(spec,) * 5, out_specs=(spec, spec), check_vma=False
    )
```

```python
import functools

import jax
import jax.numpy as jnp
from jax import lax
from jax.experimental import pallas as pl
from jax.experimental.pallas import tpu as pltpu
from jax.sharding import PartitionSpec as P

radial_weight = 8.0
azimuth_weight = 0.25
axial_weight = 0.25
flow_weight = 0.5
mass_weight = 1.0
heat_weight = 0.25
arrhenius_exponent = 2.0
slope_weight = 2.0

MESH = pl.DeviceIdType.MESH
LANES = 128
SUB = 8


def kernel(
    segments,
    sectors,
    heat_hbm,
    size_hbm,
    flux_hbm,
    goal_hbm,
    start_hbm,
    adjoint_hbm,
    sens_hbm,
    heat,
    size,
    flux,
    goal,
    state,
    inv,
    qa,
    rb,
    rhs,
    part,
    out_x,
    out_s,
    halo_out,
    halo_in,
    coef_out,
    coef_in,
    u_out,
    u_in,
    ret_out,
    ret_in,
    factor,
    side_a,
    side_b,
    in_sem,
    out_sem,
    halo_ssem,
    halo_rsem,
    coef_ssem,
    coef_rsem,
    u_ssem,
    u_rsem,
    ret_ssem,
    ret_rsem,
):
    rows, width, axial = heat.shape
    groups = width // SUB
    chunks = axial // LANES
    per_chunk = segments // chunks
    tile_rows = width // (2 * per_chunk)
    inner, outer = tuple(range(1, groups - 1)), (0, groups - 1)
    halves = (inner, outer)
    total = rows * segments
    stiffness = radial_weight * rows * rows

    seg = lax.axis_index("rad")
    sec = lax.axis_index("azi")
    above = lax.rem(sec + 1, sectors)
    below = lax.rem(sec + sectors - 1, sectors)
    peers = [lax.rem(seg + k, segments) for k in range(1, segments)]
    first = seg * rows

    span = rows // 2
    loads = [
        [
            pltpu.make_async_copy(
                src.at[pl.ds(part_of * span, span)],
                dst.at[pl.ds(part_of * span, span)],
                in_sem.at[n, part_of],
            )
            for part_of in range(2)
        ]
        for n, (src, dst) in enumerate(
            (
                (start_hbm, state),
                (heat_hbm, heat),
                (size_hbm, size),
                (flux_hbm, flux),
                (goal_hbm, goal),
            )
        )
    ]
    for load in loads:
        for copy in load:
            copy.start()

    def await_load(load):
        for copy in load:
            copy.wait()

    barrier = pltpu.get_barrier_semaphore()
    for peer in peers:
        pl.semaphore_signal(barrier, inc=1, device_id=(peer, sec), device_id_type=MESH)
    for near in (above, below):
        pl.semaphore_signal(barrier, inc=1, device_id=(seg, near), device_id_type=MESH)

    def halo_copies(sweep):
        return [
            pltpu.make_async_remote_copy(
                src_ref=halo_out.at[sweep, side],
                dst_ref=halo_in.at[sweep, side],
                send_sem=halo_ssem.at[sweep, side],
                recv_sem=halo_rsem.at[sweep, side],
                device_id=(seg, near),
                device_id_type=MESH,
            )
            for side, near in ((0, above), (1, below))
        ]

    def sends(src, dst, ssem, rsem):
        return [
            pltpu.make_async_remote_copy(
                src_ref=src.at[peer],
                dst_ref=dst.at[seg],
                send_sem=ssem.at[peer],
                recv_sem=rsem.at[seg],
                device_id=(peer, sec),
                device_id_type=MESH,
            )
            for peer in peers
        ]

    def await_from(src, dst, ssem, rsem):
        for peer in peers:
            pltpu.make_async_remote_copy(
                src_ref=src.at[peer],
                dst_ref=dst.at[peer],
                send_sem=ssem.at[peer],
                recv_sem=rsem.at[peer],
                device_id=(peer, sec),
                device_id_type=MESH,
            ).wait_recv()

    def geometry(i):
        row = (first + i).astype(jnp.float32)
        radius = 1.0 + (row + 0.5) * (1.0 / total)
        low = stiffness * (1.0 + row * (1.0 / total))
        high = stiffness * (1.0 + (row + 1.0) * (1.0 / total))
        return radius, low, high

    def azimuth_coef(radius):
        return azimuth_weight / jnp.full((1, LANES), radius, jnp.float32)

    def wide(line):
        return jnp.concatenate([line] * chunks, axis=1)

    await_load(loads[0])

    def pack(i, carry):
        halo_out[0, 0, pl.ds(i, 1), :] = state[i, width - 1 : width, :]
        halo_out[0, 1, pl.ds(i, 1), :] = state[i, 0:1, :]
        return carry

    lax.fori_loop(0, rows, pack, 0, unroll=4)
    pl.semaphore_wait(barrier, segments + 1)
    halos = halo_copies(0)
    for copy in halos:
        copy.start()

    for load in loads[1:4]:
        await_load(load)

    def rows_of(g):
        return slice(g * SUB, (g + 1) * SUB)

    def pieces():
        for c in range(chunks):
            for k in range(per_chunk):
                where_rows = slice(k * tile_rows, (k + 1) * tile_rows)
                where_cols = slice(c * LANES, (c + 1) * LANES)
                yield c * per_chunk + k, where_rows, where_cols

    def scatter(slot, plane, c_first, c_last):
        for n, chosen in enumerate(halves):
            lines = jnp.concatenate([plane[rows_of(g)] for g in chosen], axis=0)
            for owner, where_rows, cols in pieces():
                if c_first * LANES <= cols.start < c_last * LANES:
                    at = cols.start - c_first * LANES
                    coef_out[owner, slot, n] = lines[where_rows, at : at + LANES]

    half = 2 * LANES
    for h in range(axial // half):
        cols = slice(h * half, (h + 1) * half)

        def eliminate(i, carry):
            ratio, ea, prod, va, _ = carry
            radius, low, high = geometry(i)
            az2 = 2.0 * azimuth_coef(radius)
            az2 = jnp.concatenate([az2, az2], axis=1)
            viscosity = jnp.exp(
                arrhenius_exponent - arrhenius_exponent * heat[i, :, cols]
            )
            extent = size[i, :, cols]
            shear = (heat_weight * arrhenius_exponent) * viscosity * extent
            ahead = radius * (axial_weight + flow_weight * flux[i, :, cols])
            excess = (
                ahead + radius * (shear * extent + (mass_weight + axial_weight)) + az2
            )
            top = low * ratio + excess
            inverse = 1.0 / (top + high)
            ratio = top * inverse
            ea = (low * inverse) * ea
            upper = high * inverse
            va = va + prod * ea
            prod = prod * upper
            flux[i, :, cols] = ahead
            size[i, :, cols] = shear
            inv[i, :, cols] = inverse
            qa[i, :, cols] = ea
            return ratio, ea, prod, va, upper

        one = jnp.ones((width, half), jnp.float32)
        zero = jnp.zeros((width, half), jnp.float32)
        _, ea, _, va, upper = lax.fori_loop(
            0, rows, eliminate, (one, one, one, zero, zero), unroll=4
        )
        scatter(0, va, 2 * h, 2 * h + 2)
        scatter(1, ea, 2 * h, 2 * h + 2)
        scatter(2, upper, 2 * h, 2 * h + 2)

    coef_sends = sends(coef_out, coef_in, coef_ssem, coef_rsem)
    for copy in coef_sends:
        copy.start()
    coef_in[seg] = coef_out[seg]

    def respond(n, carry):
        q_next, r_next = carry
        i = rows - 1 - n
        _, _, high = geometry(i)
        upper = high * inv[i]
        q_next = qa[i] + upper * q_next
        r_next = upper * r_next
        qa[i] = q_next
        rb[i] = r_next
        return q_next, r_next

    lax.fori_loop(
        0,
        rows,
        respond,
        (jnp.zeros((width, axial), jnp.float32), jnp.ones((width, axial), jnp.float32)),
        unroll=4,
    )

    await_load(loads[4])
    sub = lax.broadcasted_iota(jnp.int32, (SUB, axial), 0)
    lane = lax.broadcasted_iota(jnp.int32, (SUB, axial), 1)

    def right_side(sweep, half):
        chosen = halves[half]

        def step(i, carry):
            radius, _, _ = geometry(i)
            az = wide(azimuth_coef(radius))
            rolled_up, rolled_down, new = {}, {}, []

            def block(g):
                return state[i, g * SUB : (g + 1) * SUB, :]

            def up(g):
                if g < 0:
                    return jnp.broadcast_to(
                        halo_in[sweep, 0, pl.ds(i, 1), :], (SUB, axial)
                    )
                if g not in rolled_up:
                    rolled_up[g] = pltpu.roll(block(g), 1, 0)
                return rolled_up[g]

            def down(g):
                if g >= groups:
                    return jnp.broadcast_to(
                        halo_in[sweep, 1, pl.ds(i, 1), :], (SUB, axial)
                    )
                if g not in rolled_down:
                    rolled_down[g] = pltpu.roll(block(g), SUB - 1, 0)
                return rolled_down[g]

            for g, (u_first, u_last) in zip(chosen, carry):
                here = slice(g * SUB, (g + 1) * SUB)
                x = block(g)
                sides = jnp.where(sub == 0, up(g - 1), up(g)) + jnp.where(
                    sub == SUB - 1, down(g + 1), down(g)
                )
                before = jnp.where(lane == 0, 0.0, pltpu.roll(x, 1, 1))
                after = jnp.where(lane == axial - 1, 0.0, pltpu.roll(x, axial - 1, 1))
                value = (
                    radius * (goal[i, here, :] + mass_weight * x + axial_weight * before)
                    + flux[i, here, :] * after
                    + az * sides
                )
                rhs[i, here, :] = value
                new.append(
                    (u_first + qa[i, here, :] * value, u_last + rb[i, here, :] * value)
                )
            return tuple(new)

        zero = jnp.zeros((SUB, axial), jnp.float32)
        sums = lax.fori_loop(0, rows, step, tuple((zero, zero) for _ in chosen), unroll=2)
        for slot in range(2):
            lines = jnp.concatenate([pair[slot] for pair in sums], axis=0)
            for owner, where_rows, cols in pieces():
                u_out[sweep, half, owner, slot] = lines[where_rows, cols]

    def send_ends(sweep, half):
        at = (sweep, half)
        copies = sends(u_out.at[at], u_in.at[at], u_ssem.at[at], u_rsem.at[at])
        for copy in copies:
            copy.start()
        u_in[sweep, half, seg] = u_out[sweep, half, seg]
        return copies

    def await_ends(sweep, half):
        at = (sweep, half)
        await_from(u_out.at[at], u_in.at[at], u_ssem.at[at], u_rsem.at[at])

    def substitute(half):
        chosen = halves[half]

        def forward(i, carry):
            _, low, _ = geometry(i)
            new = []
            for g, before in zip(chosen, carry):
                here = rows_of(g)
                now = inv[i, here, :] * (rhs[i, here, :] + low * before)
                rhs[i, here, :] = now
                new.append(now)
            return tuple(new)

        def backward(n, carry):
            i = rows - 1 - n
            _, _, high = geometry(i)
            new = []
            for g, after in zip(chosen, carry):
                here = rows_of(g)
                now = rhs[i, here, :] + (high * inv[i, here, :]) * after
                part[i, here, :] = now
                new.append(now)
            return tuple(new)

        zero = tuple(jnp.zeros((SUB, axial), jnp.float32) for _ in chosen)
        lax.fori_loop(0, rows, forward, zero, unroll=4)
        lax.fori_loop(0, rows, backward, zero, unroll=4)

    def reduced_factors(half):
        beta = None
        for s in range(segments):
            v_first, v_last, w_last = [coef_in[s, slot, half] for slot in range(3)]
            w_first = v_last * ((segments + s + 1.0) / (segments + s))
            if s == 0:
                beta = w_last
                factor[half, s, 3] = beta
                continue
            scale = 1.0 / (1.0 - v_first * beta)
            q = scale * w_first
            cross = v_last * beta
            beta = w_last + cross * q
            for slot, plane in enumerate((scale, scale * v_first, q, beta, cross)):
                factor[half, s, slot] = plane

    def reduced_solve(sweep, half):
        firsts, lasts = [], []
        for s in range(segments):
            end = [u_in[sweep, half, s, slot] for slot in range(2)]
            u_first = end[0] * (segments / (stiffness * (segments + s)))
            u_last = end[1] * (segments / (stiffness * (segments + s + 1)))
            if s == 0:
                firsts.append(u_first)
                lasts.append(u_last)
                continue
            p = factor[half, s, 0] * u_first + factor[half, s, 1] * lasts[s - 1]
            firsts.append(p)
            lasts.append(
                u_last + coef_in[s, 1, half] * lasts[s - 1] + factor[half, s, 4] * p
            )
        beyond = jnp.zeros((tile_rows, LANES), jnp.float32)
        ret_out[sweep, half, 0, 0] = beyond
        for s in range(segments - 1, -1, -1):
            ret_out[sweep, half, s, 1] = beyond
            if s < segments - 1:
                ret_out[sweep, half, s + 1, 0] = lasts[s] + factor[half, s, 3] * beyond
            if s > 0:
                beyond = firsts[s] + factor[half, s, 2] * beyond

    def send_back(sweep, half):
        at = (sweep, half)
        copies = sends(ret_out.at[at], ret_in.at[at], ret_ssem.at[at], ret_rsem.at[at])
        for copy in copies:
            copy.start()
        ret_in[sweep, half, seg] = ret_out[sweep, half, seg]
        return copies

    def ends(sweep, half):
        at = (sweep, half)
        await_from(ret_out.at[at], ret_in.at[at], ret_ssem.at[at], ret_rsem.at[at])
        for owner, where_rows, cols in pieces():
            side_a[half, where_rows, cols] = ret_in[sweep, half, owner, 0]
            side_b[half, where_rows, cols] = ret_in[sweep, half, owner, 1]
        return [
            (side_a[half, rows_of(n), :], side_b[half, rows_of(n), :])
            for n in range(len(halves[half]))
        ]

    def solved(i, half, sides):
        for g, (a, b) in zip(halves[half], sides):
            here = rows_of(g)
            yield g, part[i, here, :] + qa[i, here, :] * a + rb[i, here, :] * b

    for copy in halos:
        copy.wait_recv()
    started = [coef_sends, halos]
    for half in (1, 0):
        right_side(0, half)
        started.append(send_ends(0, half))
    await_from(coef_out, coef_in, coef_ssem, coef_rsem)
    for half in (1, 0):
        reduced_factors(half)
    for half in (1, 0):
        substitute(half)
        await_ends(0, half)
        reduced_solve(0, half)
        started.append(send_back(0, half))

    last_lane = lax.broadcasted_iota(jnp.int32, (width, axial), 1) == axial - 1

    def slope(i, carry):
        here = heat[i]
        rise = jnp.where(last_lane, 0.0, pltpu.roll(here, axial - 1, 1) - here)
        heat[i] = slope_weight * rise - size[i]
        return carry

    lax.fori_loop(0, rows, slope, 0, unroll=4)

    for half in (1, 0):
        sides = ends(0, half)

        def advance(i, carry):
            for g, x in solved(i, half, sides):
                state[i, rows_of(g), :] = x
                if g == groups - 1:
                    halo_out[1, 0, pl.ds(i, 1), :] = x[SUB - 1 : SUB, :]
                if g == 0:
                    halo_out[1, 1, pl.ds(i, 1), :] = x[0:1, :]
            return carry

        lax.fori_loop(0, rows, advance, 0, unroll=4)
        if half == 1:
            halos = halo_copies(1)
            started.append(halos)
            for copy in halos:
                copy.start()

    for half in (0, 1):
        if half == 1:
            for copy in halos:
                copy.wait_recv()
        right_side(1, half)
        started.append(send_ends(1, half))
    for half in (0, 1):
        substitute(half)
        await_ends(1, half)
        reduced_solve(1, half)
        started.append(send_back(1, half))

    stores = []
    for half in (0, 1):
        sides = ends(1, half)

        def finish(i, carry):
            for g, x in solved(i, half, sides):
                here = rows_of(g)
                out_x[i, here, :] = x
                out_s[i, here, :] = x * heat[i, here, :]
            return carry

        lax.fori_loop(0, rows, finish, 0, unroll=4)
        for g in halves[half]:
            here = pl.ds(g * SUB, SUB)
            for m, (src, dst) in enumerate(((out_x, adjoint_hbm), (out_s, sens_hbm))):
                store = pltpu.make_async_copy(
                    src.at[:, here], dst.at[:, here], out_sem.at[m, g]
                )
                store.start()
                stores.append(store)

    for copies in started:
        for copy in copies:
            copy.wait_send()
    for store in stores:
        store.wait()


def deliver(adjoint, sens, adjoint_out, sens_out, sem):
    parts = sem.shape[1]
    span = adjoint.shape[0] // parts
    copies = []
    for n in range(parts):
        at = pl.ds(n * span, span)
        for m, (src, dst) in enumerate(((adjoint, adjoint_out), (sens, sens_out))):
            copies.append(pltpu.make_async_copy(src.at[at], dst.at[at], sem.at[m, n]))
    for copy in copies:
        copy.start()
    for copy in copies:
        copy.wait()


def solution(mesh):
    segments, sectors = mesh.shape["rad"], mesh.shape["azi"]
    spec = P("rad", "azi", None)

    def body(heat, size, flux, goal, start):
        rows, width, axial = heat.shape
        half_rows = width // 2
        tile_rows = half_rows * axial // (segments * LANES)
        block = pltpu.VMEM((rows, width, axial), jnp.float32)
        tile = (tile_rows, LANES)
        shape = jax.ShapeDtypeStruct((rows, width, axial), jnp.float32)
        dma = pltpu.SemaphoreType.DMA
        cells = rows * width * axial
        adjoint, sens = pl.pallas_call(
            functools.partial(kernel, segments, sectors),
            out_shape=(shape, shape),
            in_specs=[pl.BlockSpec(memory_space=pltpu.HBM)] * 5,
            out_specs=[pl.BlockSpec(memory_space=pl.ANY)] * 2,
            scratch_shapes=[block] * 12
            + [
                pltpu.VMEM((2, 2, rows, axial), jnp.float32),
                pltpu.VMEM((2, 2, rows, axial), jnp.float32),
                pltpu.VMEM((segments, 3, 2) + tile, jnp.float32),
                pltpu.VMEM((segments, 3, 2) + tile, jnp.float32),
                pltpu.VMEM((2, 2, segments, 2) + tile, jnp.float32),
                pltpu.VMEM((2, 2, segments, 2) + tile, jnp.float32),
                pltpu.VMEM((2, 2, segments, 2) + tile, jnp.float32),
                pltpu.VMEM((2, 2, segments, 2) + tile, jnp.float32),
                pltpu.VMEM((2, segments, 5) + tile, jnp.float32),
                pltpu.VMEM((2, half_rows, axial), jnp.float32),
                pltpu.VMEM((2, half_rows, axial), jnp.float32),
                dma((5, 2)),
                dma((2, width // SUB)),
                dma((2, 2)),
                dma((2, 2)),
                dma((segments,)),
                dma((segments,)),
                dma((2, 2, segments)),
                dma((2, 2, segments)),
                dma((2, 2, segments)),
                dma((2, 2, segments)),
            ],
            compiler_params=pltpu.CompilerParams(
                collective_id=0, has_side_effects=True, vmem_limit_bytes=60 * 2**20
            ),
            cost_estimate=pl.CostEstimate(
                flops=120 * cells, bytes_accessed=28 * cells, transcendentals=2 * cells
            ),
        )(heat, size, flux, goal, start)
        return pl.pallas_call(
            deliver,
            out_shape=(shape, shape),
            in_specs=[pl.BlockSpec(memory_space=pl.ANY)] * 2,
            out_specs=[pl.BlockSpec(memory_space=pl.ANY)] * 2,
            scratch_shapes=[dma((2, 4))],
            compiler_params=pltpu.CompilerParams(vmem_limit_bytes=60 * 2**20),
            cost_estimate=pl.CostEstimate(
                flops=0, bytes_accessed=16 * cells, transcendentals=0
            ),
        )(adjoint, sens)

    return jax.shard_map(
        body, mesh=mesh, in_specs=(spec,) * 5, out_specs=(spec, spec), check_vma=False
    )
```

```python
import functools

import jax
import jax.numpy as jnp
from jax import lax
from jax.experimental import pallas as pl
from jax.experimental.pallas import tpu as pltpu
from jax.sharding import PartitionSpec as P

radial_weight = 8.0
azimuth_weight = 0.25
axial_weight = 0.25
flow_weight = 0.5
mass_weight = 1.0
heat_weight = 0.25
arrhenius_exponent = 2.0
slope_weight = 2.0

MESH = pl.DeviceIdType.MESH
LANES = 128
SUB = 8


def kernel(
    segments,
    sectors,
    heat_hbm,
    size_hbm,
    flux_hbm,
    goal_hbm,
    start_hbm,
    adjoint_hbm,
    sens_hbm,
    heat,
    size,
    flux,
    goal,
    state,
    inv,
    qa,
    rb,
    rhs,
    part,
    out_x,
    out_s,
    halo_out,
    halo_in,
    coef_out,
    coef_in,
    u_out,
    u_in,
    ret_out,
    ret_in,
    factor,
    side_a,
    side_b,
    in_sem,
    out_sem,
    halo_ssem,
    halo_rsem,
    coef_ssem,
    coef_rsem,
    u_ssem,
    u_rsem,
    ret_ssem,
    ret_rsem,
):
    rows, width, axial = heat.shape
    groups = width // SUB
    chunks = axial // LANES
    per_chunk = segments // chunks
    tile_rows = width // (2 * per_chunk)
    inner, outer = tuple(range(1, groups - 1)), (0, groups - 1)
    halves = (inner, outer)
    total = rows * segments
    stiffness = radial_weight * rows * rows

    seg = lax.axis_index("rad")
    sec = lax.axis_index("azi")
    above = lax.rem(sec + 1, sectors)
    below = lax.rem(sec + sectors - 1, sectors)
    peers = [lax.rem(seg + k, segments) for k in range(1, segments)]
    first = seg * rows

    span = rows // 2
    loads = [
        [
            pltpu.make_async_copy(
                src.at[pl.ds(part_of * span, span)],
                dst.at[pl.ds(part_of * span, span)],
                in_sem.at[n, part_of],
            )
            for part_of in range(2)
        ]
        for n, (src, dst) in enumerate(
            (
                (start_hbm, state),
                (heat_hbm, heat),
                (size_hbm, size),
                (flux_hbm, flux),
                (goal_hbm, goal),
            )
        )
    ]
    for load in loads:
        for copy in load:
            copy.start()

    def await_load(load):
        for copy in load:
            copy.wait()

    barrier = pltpu.get_barrier_semaphore()
    for peer in peers:
        pl.semaphore_signal(barrier, inc=1, device_id=(peer, sec), device_id_type=MESH)
    for near in (above, below):
        pl.semaphore_signal(barrier, inc=1, device_id=(seg, near), device_id_type=MESH)

    def halo_copies(sweep):
        return [
            pltpu.make_async_remote_copy(
                src_ref=halo_out.at[sweep, side],
                dst_ref=halo_in.at[sweep, side],
                send_sem=halo_ssem.at[sweep, side],
                recv_sem=halo_rsem.at[sweep, side],
                device_id=(seg, near),
                device_id_type=MESH,
            )
            for side, near in ((0, above), (1, below))
        ]

    def sends(src, dst, ssem, rsem):
        return [
            pltpu.make_async_remote_copy(
                src_ref=src.at[peer],
                dst_ref=dst.at[seg],
                send_sem=ssem.at[peer],
                recv_sem=rsem.at[seg],
                device_id=(peer, sec),
                device_id_type=MESH,
            )
            for peer in peers
        ]

    def await_from(src, dst, ssem, rsem):
        for peer in peers:
            pltpu.make_async_remote_copy(
                src_ref=src.at[peer],
                dst_ref=dst.at[peer],
                send_sem=ssem.at[peer],
                recv_sem=rsem.at[peer],
                device_id=(peer, sec),
                device_id_type=MESH,
            ).wait_recv()

    def geometry(i):
        row = (first + i).astype(jnp.float32)
        radius = 1.0 + (row + 0.5) * (1.0 / total)
        low = stiffness * (1.0 + row * (1.0 / total))
        high = stiffness * (1.0 + (row + 1.0) * (1.0 / total))
        return radius, low, high

    def azimuth_coef(radius):
        return azimuth_weight / jnp.full((1, LANES), radius, jnp.float32)

    def wide(line):
        return jnp.concatenate([line] * chunks, axis=1)

    await_load(loads[0])

    def pack(i, carry):
        halo_out[0, 0, pl.ds(i, 1), :] = state[i, width - 1 : width, :]
        halo_out[0, 1, pl.ds(i, 1), :] = state[i, 0:1, :]
        return carry

    lax.fori_loop(0, rows, pack, 0, unroll=4)
    pl.semaphore_wait(barrier, segments + 1)
    halos = halo_copies(0)
    for copy in halos:
        copy.start()

    for load in loads[1:4]:
        await_load(load)

    def rows_of(g):
        return slice(g * SUB, (g + 1) * SUB)

    def pieces():
        for c in range(chunks):
            for k in range(per_chunk):
                where_rows = slice(k * tile_rows, (k + 1) * tile_rows)
                where_cols = slice(c * LANES, (c + 1) * LANES)
                yield c * per_chunk + k, where_rows, where_cols

    def scatter(slot, plane, c_first, c_last):
        for n, chosen in enumerate(halves):
            lines = jnp.concatenate([plane[rows_of(g)] for g in chosen], axis=0)
            for owner, where_rows, cols in pieces():
                if c_first * LANES <= cols.start < c_last * LANES:
                    at = cols.start - c_first * LANES
                    coef_out[owner, slot, n] = lines[where_rows, at : at + LANES]

    half = 2 * LANES
    for h in range(axial // half):
        cols = slice(h * half, (h + 1) * half)

        def eliminate(i, carry):
            ratio, ea, prod, va, _ = carry
            radius, low, high = geometry(i)
            az2 = 2.0 * azimuth_coef(radius)
            az2 = jnp.concatenate([az2, az2], axis=1)
            viscosity = jnp.exp(
                arrhenius_exponent - arrhenius_exponent * heat[i, :, cols]
            )
            extent = size[i, :, cols]
            shear = (heat_weight * arrhenius_exponent) * viscosity * extent
            ahead = radius * (axial_weight + flow_weight * flux[i, :, cols])
            excess = (
                ahead + radius * (shear * extent + (mass_weight + axial_weight)) + az2
            )
            top = low * ratio + excess
            inverse = 1.0 / (top + high)
            ratio = top * inverse
            ea = (low * inverse) * ea
            upper = high * inverse
            va = va + prod * ea
            prod = prod * upper
            flux[i, :, cols] = ahead
            size[i, :, cols] = shear
            inv[i, :, cols] = inverse
            qa[i, :, cols] = ea
            return ratio, ea, prod, va, upper

        one = jnp.ones((width, half), jnp.float32)
        zero = jnp.zeros((width, half), jnp.float32)
        _, ea, _, va, upper = lax.fori_loop(
            0, rows, eliminate, (one, one, one, zero, zero), unroll=4
        )
        scatter(0, va, 2 * h, 2 * h + 2)
        scatter(1, ea, 2 * h, 2 * h + 2)
        scatter(2, upper, 2 * h, 2 * h + 2)

    coef_sends = sends(coef_out, coef_in, coef_ssem, coef_rsem)
    for copy in coef_sends:
        copy.start()
    coef_in[seg] = coef_out[seg]

    def respond(n, carry):
        q_next, r_next = carry
        i = rows - 1 - n
        _, _, high = geometry(i)
        upper = high * inv[i]
        q_next = qa[i] + upper * q_next
        r_next = upper * r_next
        qa[i] = q_next
        rb[i] = r_next
        return q_next, r_next

    lax.fori_loop(
        0,
        rows,
        respond,
        (jnp.zeros((width, axial), jnp.float32), jnp.ones((width, axial), jnp.float32)),
        unroll=4,
    )

    await_load(loads[4])
    sub = lax.broadcasted_iota(jnp.int32, (SUB, axial), 0)
    lane = lax.broadcasted_iota(jnp.int32, (SUB, axial), 1)

    def right_side(sweep, half):
        chosen = halves[half]

        def step(i, carry):
            radius, _, _ = geometry(i)
            az = wide(azimuth_coef(radius))
            rolled_up, rolled_down, new = {}, {}, []

            def block(g):
                return state[i, g * SUB : (g + 1) * SUB, :]

            def up(g):
                if g < 0:
                    return jnp.broadcast_to(
                        halo_in[sweep, 0, pl.ds(i, 1), :], (SUB, axial)
                    )
                if g not in rolled_up:
                    rolled_up[g] = pltpu.roll(block(g), 1, 0)
                return rolled_up[g]

            def down(g):
                if g >= groups:
                    return jnp.broadcast_to(
                        halo_in[sweep, 1, pl.ds(i, 1), :], (SUB, axial)
                    )
                if g not in rolled_down:
                    rolled_down[g] = pltpu.roll(block(g), SUB - 1, 0)
                return rolled_down[g]

            for g, (u_first, u_last) in zip(chosen, carry):
                here = slice(g * SUB, (g + 1) * SUB)
                x = block(g)
                sides = jnp.where(sub == 0, up(g - 1), up(g)) + jnp.where(
                    sub == SUB - 1, down(g + 1), down(g)
                )
                before = jnp.where(lane == 0, 0.0, pltpu.roll(x, 1, 1))
                after = jnp.where(lane == axial - 1, 0.0, pltpu.roll(x, axial - 1, 1))
                value = (
                    radius * (goal[i, here, :] + mass_weight * x + axial_weight * before)
                    + flux[i, here, :] * after
                    + az * sides
                )
                rhs[i, here, :] = value
                new.append(
                    (u_first + qa[i, here, :] * value, u_last + rb[i, here, :] * value)
                )
            return tuple(new)

        zero = jnp.zeros((SUB, axial), jnp.float32)
        sums = lax.fori_loop(0, rows, step, tuple((zero, zero) for _ in chosen), unroll=2)
        for slot in range(2):
            lines = jnp.concatenate([pair[slot] for pair in sums], axis=0)
            for owner, where_rows, cols in pieces():
                u_out[sweep, half, owner, slot] = lines[where_rows, cols]

    def send_ends(sweep, half):
        at = (sweep, half)
        copies = sends(u_out.at[at], u_in.at[at], u_ssem.at[at], u_rsem.at[at])
        for copy in copies:
            copy.start()
        u_in[sweep, half, seg] = u_out[sweep, half, seg]
        return copies

    def await_ends(sweep, half):
        at = (sweep, half)
        await_from(u_out.at[at], u_in.at[at], u_ssem.at[at], u_rsem.at[at])

    def substitute(half):
        chosen = halves[half]

        def forward(i, carry):
            _, low, _ = geometry(i)
            new = []
            for g, before in zip(chosen, carry):
                here = rows_of(g)
                now = inv[i, here, :] * (rhs[i, here, :] + low * before)
                rhs[i, here, :] = now
                new.append(now)
            return tuple(new)

        def backward(n, carry):
            i = rows - 1 - n
            _, _, high = geometry(i)
            new = []
            for g, after in zip(chosen, carry):
                here = rows_of(g)
                now = rhs[i, here, :] + (high * inv[i, here, :]) * after
                part[i, here, :] = now
                new.append(now)
            return tuple(new)

        zero = tuple(jnp.zeros((SUB, axial), jnp.float32) for _ in chosen)
        lax.fori_loop(0, rows, forward, zero, unroll=4)
        lax.fori_loop(0, rows, backward, zero, unroll=4)

    def reduced_factors(half):
        beta = None
        for s in range(segments):
            v_first, v_last, w_last = [coef_in[s, slot, half] for slot in range(3)]
            w_first = v_last * ((segments + s + 1.0) / (segments + s))
            if s == 0:
                beta = w_last
                factor[half, s, 3] = beta
                continue
            scale = 1.0 / (1.0 - v_first * beta)
            q = scale * w_first
            cross = v_last * beta
            beta = w_last + cross * q
            for slot, plane in enumerate((scale, scale * v_first, q, beta, cross)):
                factor[half, s, slot] = plane

    def reduced_solve(sweep, half):
        firsts, lasts = [], []
        for s in range(segments):
            end = [u_in[sweep, half, s, slot] for slot in range(2)]
            u_first = end[0] * (segments / (stiffness * (segments + s)))
            u_last = end[1] * (segments / (stiffness * (segments + s + 1)))
            if s == 0:
                firsts.append(u_first)
                lasts.append(u_last)
                continue
            p = factor[half, s, 0] * u_first + factor[half, s, 1] * lasts[s - 1]
            firsts.append(p)
            lasts.append(
                u_last + coef_in[s, 1, half] * lasts[s - 1] + factor[half, s, 4] * p
            )
        beyond = jnp.zeros((tile_rows, LANES), jnp.float32)
        ret_out[sweep, half, 0, 0] = beyond
        for s in range(segments - 1, -1, -1):
            ret_out[sweep, half, s, 1] = beyond
            if s < segments - 1:
                ret_out[sweep, half, s + 1, 0] = lasts[s] + factor[half, s, 3] * beyond
            if s > 0:
                beyond = firsts[s] + factor[half, s, 2] * beyond

    def send_back(sweep, half):
        at = (sweep, half)
        copies = sends(ret_out.at[at], ret_in.at[at], ret_ssem.at[at], ret_rsem.at[at])
        for copy in copies:
            copy.start()
        ret_in[sweep, half, seg] = ret_out[sweep, half, seg]
        return copies

    def ends(sweep, half):
        at = (sweep, half)
        await_from(ret_out.at[at], ret_in.at[at], ret_ssem.at[at], ret_rsem.at[at])
        for owner, where_rows, cols in pieces():
            side_a[half, where_rows, cols] = ret_in[sweep, half, owner, 0]
            side_b[half, where_rows, cols] = ret_in[sweep, half, owner, 1]
        return [
            (side_a[half, rows_of(n), :], side_b[half, rows_of(n), :])
            for n in range(len(halves[half]))
        ]

    def solved(i, half, sides):
        for g, (a, b) in zip(halves[half], sides):
            here = rows_of(g)
            yield g, part[i, here, :] + qa[i, here, :] * a + rb[i, here, :] * b

    for copy in halos:
        copy.wait_recv()
    started = [coef_sends, halos]
    for half in (1, 0):
        right_side(0, half)
        started.append(send_ends(0, half))
    await_from(coef_out, coef_in, coef_ssem, coef_rsem)
    for half in (1, 0):
        reduced_factors(half)
    for half in (1, 0):
        substitute(half)
        await_ends(0, half)
        reduced_solve(0, half)
        started.append(send_back(0, half))

    last_lane = lax.broadcasted_iota(jnp.int32, (width, axial), 1) == axial - 1

    def slope(i, carry):
        here = heat[i]
        rise = jnp.where(last_lane, 0.0, pltpu.roll(here, axial - 1, 1) - here)
        heat[i] = slope_weight * rise - size[i]
        return carry

    lax.fori_loop(0, rows, slope, 0, unroll=4)

    for half in (1, 0):
        sides = ends(0, half)

        def advance(i, carry):
            for g, x in solved(i, half, sides):
                state[i, rows_of(g), :] = x
                if g == groups - 1:
                    halo_out[1, 0, pl.ds(i, 1), :] = x[SUB - 1 : SUB, :]
                if g == 0:
                    halo_out[1, 1, pl.ds(i, 1), :] = x[0:1, :]
            return carry

        lax.fori_loop(0, rows, advance, 0, unroll=4)
        if half == 1:
            halos = halo_copies(1)
            started.append(halos)
            for copy in halos:
                copy.start()

    for half in (0, 1):
        if half == 1:
            for copy in halos:
                copy.wait_recv()
        right_side(1, half)
        started.append(send_ends(1, half))
    for half in (0, 1):
        substitute(half)
        await_ends(1, half)
        reduced_solve(1, half)
        started.append(send_back(1, half))

    stores = []
    for half in (0, 1):
        sides = ends(1, half)

        def finish(i, carry):
            for g, x in solved(i, half, sides):
                here = rows_of(g)
                out_x[i, here, :] = x
                out_s[i, here, :] = x * heat[i, here, :]
            return carry

        lax.fori_loop(0, rows, finish, 0, unroll=4)
        for g in halves[half]:
            here = pl.ds(g * SUB, SUB)
            for m, (src, dst) in enumerate(((out_x, adjoint_hbm), (out_s, sens_hbm))):
                store = pltpu.make_async_copy(
                    src.at[:, here], dst.at[:, here], out_sem.at[m, g]
                )
                store.start()
                stores.append(store)

    for copies in started:
        for copy in copies:
            copy.wait_send()
    for store in stores:
        store.wait()


def deliver(adjoint, sens, adjoint_out, sens_out, sem):
    parts = sem.shape[1]
    span = adjoint.shape[0] // parts
    copies = []
    for n in range(parts):
        at = pl.ds(n * span, span)
        for m, (src, dst) in enumerate(((adjoint, adjoint_out), (sens, sens_out))):
            copies.append(pltpu.make_async_copy(src.at[at], dst.at[at], sem.at[m, n]))
    for copy in copies:
        copy.start()
    for copy in copies:
        copy.wait()


def solution(mesh):
    segments, sectors = mesh.shape["rad"], mesh.shape["azi"]
    spec = P("rad", "azi", None)

    def body(heat, size, flux, goal, start):
        rows, width, axial = heat.shape
        half_rows = width // 2
        tile_rows = half_rows * axial // (segments * LANES)
        block = pltpu.VMEM((rows, width, axial), jnp.float32)
        tile = (tile_rows, LANES)
        shape = jax.ShapeDtypeStruct((rows, width, axial), jnp.float32)
        dma = pltpu.SemaphoreType.DMA
        cells = rows * width * axial
        adjoint, sens = pl.pallas_call(
            functools.partial(kernel, segments, sectors),
            out_shape=(shape, shape),
            in_specs=[pl.BlockSpec(memory_space=pltpu.HBM)] * 5,
            out_specs=[pl.BlockSpec(memory_space=pl.ANY)] * 2,
            scratch_shapes=[block] * 12
            + [
                pltpu.VMEM((2, 2, rows, axial), jnp.float32),
                pltpu.VMEM((2, 2, rows, axial), jnp.float32),
                pltpu.VMEM((segments, 3, 2) + tile, jnp.float32),
                pltpu.VMEM((segments, 3, 2) + tile, jnp.float32),
                pltpu.VMEM((2, 2, segments, 2) + tile, jnp.float32),
                pltpu.VMEM((2, 2, segments, 2) + tile, jnp.float32),
                pltpu.VMEM((2, 2, segments, 2) + tile, jnp.float32),
                pltpu.VMEM((2, 2, segments, 2) + tile, jnp.float32),
                pltpu.VMEM((2, segments, 5) + tile, jnp.float32),
                pltpu.VMEM((2, half_rows, axial), jnp.float32),
                pltpu.VMEM((2, half_rows, axial), jnp.float32),
                dma((5, 2)),
                dma((2, width // SUB)),
                dma((2, 2)),
                dma((2, 2)),
                dma((segments,)),
                dma((segments,)),
                dma((2, 2, segments)),
                dma((2, 2, segments)),
                dma((2, 2, segments)),
                dma((2, 2, segments)),
            ],
            compiler_params=pltpu.CompilerParams(
                collective_id=0, has_side_effects=True, vmem_limit_bytes=51 * 2**20
            ),
            cost_estimate=pl.CostEstimate(
                flops=120 * cells, bytes_accessed=28 * cells, transcendentals=2 * cells
            ),
        )(heat, size, flux, goal, start)
        return pl.pallas_call(
            deliver,
            out_shape=(shape, shape),
            in_specs=[pl.BlockSpec(memory_space=pl.ANY)] * 2,
            out_specs=[pl.BlockSpec(memory_space=pl.ANY)] * 2,
            scratch_shapes=[dma((2, 4))],
            compiler_params=pltpu.CompilerParams(vmem_limit_bytes=2**20),
            cost_estimate=pl.CostEstimate(
                flops=0, bytes_accessed=16 * cells, transcendentals=0
            ),
        )(adjoint, sens)

    return jax.shard_map(
        body, mesh=mesh, in_specs=(spec,) * 5, out_specs=(spec, spec), check_vma=False
    )
```

```python
import functools

import jax
import jax.numpy as jnp
from jax import lax
from jax.experimental import pallas as pl
from jax.experimental.pallas import tpu as pltpu
from jax.sharding import PartitionSpec as P

radial_weight = 8.0
azimuth_weight = 0.25
axial_weight = 0.25
flow_weight = 0.5
mass_weight = 1.0
heat_weight = 0.25
arrhenius_exponent = 2.0
slope_weight = 2.0

MESH = pl.DeviceIdType.MESH
LANES = 128
SUB = 8


def kernel(
    segments,
    sectors,
    heat_hbm,
    size_hbm,
    flux_hbm,
    goal_hbm,
    start_hbm,
    adjoint_hbm,
    sens_hbm,
    heat,
    size,
    flux,
    goal,
    state,
    inv,
    qa,
    rb,
    rhs,
    part,
    out_x,
    out_s,
    halo_out,
    halo_in,
    coef_out,
    coef_in,
    u_out,
    u_in,
    ret_out,
    ret_in,
    factor,
    side_a,
    side_b,
    in_sem,
    out_sem,
    halo_ssem,
    halo_rsem,
    coef_ssem,
    coef_rsem,
    u_ssem,
    u_rsem,
    ret_ssem,
    ret_rsem,
):
    rows, width, axial = heat.shape
    groups = width // SUB
    chunks = axial // LANES
    per_chunk = segments // chunks
    tile_rows = width // (2 * per_chunk)
    inner, outer = tuple(range(1, groups - 1)), (0, groups - 1)
    halves = (inner, outer)
    total = rows * segments
    stiffness = radial_weight * rows * rows

    seg = lax.axis_index("rad")
    sec = lax.axis_index("azi")
    above = lax.rem(sec + 1, sectors)
    below = lax.rem(sec + sectors - 1, sectors)
    peers = [lax.rem(seg + k, segments) for k in range(1, segments)]
    first = seg * rows

    span = rows // 2
    loads = [
        [
            pltpu.make_async_copy(
                src.at[pl.ds(part_of * span, span)],
                dst.at[pl.ds(part_of * span, span)],
                in_sem.at[n, part_of],
            )
            for part_of in range(2)
        ]
        for n, (src, dst) in enumerate(
            (
                (start_hbm, state),
                (heat_hbm, heat),
                (size_hbm, size),
                (flux_hbm, flux),
                (goal_hbm, goal),
            )
        )
    ]
    for load in loads:
        for copy in load:
            copy.start()

    def await_load(load):
        for copy in load:
            copy.wait()

    barrier = pltpu.get_barrier_semaphore()
    for peer in peers:
        pl.semaphore_signal(barrier, inc=1, device_id=(peer, sec), device_id_type=MESH)
    for near in (above, below):
        pl.semaphore_signal(barrier, inc=1, device_id=(seg, near), device_id_type=MESH)

    def halo_copies(sweep):
        return [
            pltpu.make_async_remote_copy(
                src_ref=halo_out.at[sweep, side],
                dst_ref=halo_in.at[sweep, side],
                send_sem=halo_ssem.at[sweep, side],
                recv_sem=halo_rsem.at[sweep, side],
                device_id=(seg, near),
                device_id_type=MESH,
            )
            for side, near in ((0, above), (1, below))
        ]

    def sends(src, dst, ssem, rsem):
        return [
            pltpu.make_async_remote_copy(
                src_ref=src.at[peer],
                dst_ref=dst.at[seg],
                send_sem=ssem.at[peer],
                recv_sem=rsem.at[seg],
                device_id=(peer, sec),
                device_id_type=MESH,
            )
            for peer in peers
        ]

    def await_from(src, dst, ssem, rsem):
        for peer in peers:
            pltpu.make_async_remote_copy(
                src_ref=src.at[peer],
                dst_ref=dst.at[peer],
                send_sem=ssem.at[peer],
                recv_sem=rsem.at[peer],
                device_id=(peer, sec),
                device_id_type=MESH,
            ).wait_recv()

    def geometry(i):
        row = (first + i).astype(jnp.float32)
        radius = 1.0 + (row + 0.5) * (1.0 / total)
        low = stiffness * (1.0 + row * (1.0 / total))
        high = stiffness * (1.0 + (row + 1.0) * (1.0 / total))
        return radius, low, high

    def azimuth_coef(radius):
        return azimuth_weight / jnp.full((1, LANES), radius, jnp.float32)

    def wide(line):
        return jnp.concatenate([line] * chunks, axis=1)

    await_load(loads[0])

    def pack(i, carry):
        halo_out[0, 0, pl.ds(i, 1), :] = state[i, width - 1 : width, :]
        halo_out[0, 1, pl.ds(i, 1), :] = state[i, 0:1, :]
        return carry

    lax.fori_loop(0, rows, pack, 0, unroll=4)
    pl.semaphore_wait(barrier, segments + 1)
    halos = halo_copies(0)
    for copy in halos:
        copy.start()

    for load in loads[1:4]:
        await_load(load)

    def rows_of(g):
        return slice(g * SUB, (g + 1) * SUB)

    def pieces():
        for c in range(chunks):
            for k in range(per_chunk):
                where_rows = slice(k * tile_rows, (k + 1) * tile_rows)
                where_cols = slice(c * LANES, (c + 1) * LANES)
                yield c * per_chunk + k, where_rows, where_cols

    def scatter(slot, plane, c_first, c_last):
        for n, chosen in enumerate(halves):
            lines = jnp.concatenate([plane[rows_of(g)] for g in chosen], axis=0)
            for owner, where_rows, cols in pieces():
                if c_first * LANES <= cols.start < c_last * LANES:
                    at = cols.start - c_first * LANES
                    coef_out[owner, slot, n] = lines[where_rows, at : at + LANES]

    half = 2 * LANES
    for h in range(axial // half):
        cols = slice(h * half, (h + 1) * half)

        def eliminate(i, carry):
            ratio, ea, prod, va, _ = carry
            radius, low, high = geometry(i)
            az2 = 2.0 * azimuth_coef(radius)
            az2 = jnp.concatenate([az2, az2], axis=1)
            viscosity = jnp.exp(
                arrhenius_exponent - arrhenius_exponent * heat[i, :, cols]
            )
            extent = size[i, :, cols]
            shear = (heat_weight * arrhenius_exponent) * viscosity * extent
            ahead = radius * (axial_weight + flow_weight * flux[i, :, cols])
            excess = (
                ahead + radius * (shear * extent + (mass_weight + axial_weight)) + az2
            )
            top = low * ratio + excess
            inverse = 1.0 / (top + high)
            ratio = top * inverse
            ea = (low * inverse) * ea
            upper = high * inverse
            va = va + prod * ea
            prod = prod * upper
            flux[i, :, cols] = ahead
            size[i, :, cols] = shear
            inv[i, :, cols] = inverse
            qa[i, :, cols] = ea
            return ratio, ea, prod, va, upper

        one = jnp.ones((width, half), jnp.float32)
        zero = jnp.zeros((width, half), jnp.float32)
        _, ea, _, va, upper = lax.fori_loop(
            0, rows, eliminate, (one, one, one, zero, zero), unroll=4
        )
        scatter(0, va, 2 * h, 2 * h + 2)
        scatter(1, ea, 2 * h, 2 * h + 2)
        scatter(2, upper, 2 * h, 2 * h + 2)

    coef_sends = sends(coef_out, coef_in, coef_ssem, coef_rsem)
    for copy in coef_sends:
        copy.start()
    coef_in[seg] = coef_out[seg]

    def respond(n, carry):
        q_next, r_next = carry
        i = rows - 1 - n
        _, _, high = geometry(i)
        upper = high * inv[i]
        q_next = qa[i] + upper * q_next
        r_next = upper * r_next
        qa[i] = q_next
        rb[i] = r_next
        return q_next, r_next

    lax.fori_loop(
        0,
        rows,
        respond,
        (jnp.zeros((width, axial), jnp.float32), jnp.ones((width, axial), jnp.float32)),
        unroll=4,
    )

    await_load(loads[4])
    sub = lax.broadcasted_iota(jnp.int32, (SUB, axial), 0)
    lane = lax.broadcasted_iota(jnp.int32, (SUB, axial), 1)

    def right_side(sweep, half):
        chosen = halves[half]

        def step(i, carry):
            radius, _, _ = geometry(i)
            az = wide(azimuth_coef(radius))
            rolled_up, rolled_down, new = {}, {}, []

            def block(g):
                return state[i, g * SUB : (g + 1) * SUB, :]

            def up(g):
                if g < 0:
                    return jnp.broadcast_to(
                        halo_in[sweep, 0, pl.ds(i, 1), :], (SUB, axial)
                    )
                if g not in rolled_up:
                    rolled_up[g] = pltpu.roll(block(g), 1, 0)
                return rolled_up[g]

            def down(g):
                if g >= groups:
                    return jnp.broadcast_to(
                        halo_in[sweep, 1, pl.ds(i, 1), :], (SUB, axial)
                    )
                if g not in rolled_down:
                    rolled_down[g] = pltpu.roll(block(g), SUB - 1, 0)
                return rolled_down[g]

            for g, (u_first, u_last) in zip(chosen, carry):
                here = slice(g * SUB, (g + 1) * SUB)
                x = block(g)
                sides = jnp.where(sub == 0, up(g - 1), up(g)) + jnp.where(
                    sub == SUB - 1, down(g + 1), down(g)
                )
                before = jnp.where(lane == 0, 0.0, pltpu.roll(x, 1, 1))
                after = jnp.where(lane == axial - 1, 0.0, pltpu.roll(x, axial - 1, 1))
                value = (
                    radius * (goal[i, here, :] + mass_weight * x + axial_weight * before)
                    + flux[i, here, :] * after
                    + az * sides
                )
                rhs[i, here, :] = value
                new.append(
                    (u_first + qa[i, here, :] * value, u_last + rb[i, here, :] * value)
                )
            return tuple(new)

        zero = jnp.zeros((SUB, axial), jnp.float32)
        sums = lax.fori_loop(0, rows, step, tuple((zero, zero) for _ in chosen), unroll=2)
        for slot in range(2):
            lines = jnp.concatenate([pair[slot] for pair in sums], axis=0)
            for owner, where_rows, cols in pieces():
                u_out[sweep, half, owner, slot] = lines[where_rows, cols]

    def send_ends(sweep, half):
        at = (sweep, half)
        copies = sends(u_out.at[at], u_in.at[at], u_ssem.at[at], u_rsem.at[at])
        for copy in copies:
            copy.start()
        u_in[sweep, half, seg] = u_out[sweep, half, seg]
        return copies

    def await_ends(sweep, half):
        at = (sweep, half)
        await_from(u_out.at[at], u_in.at[at], u_ssem.at[at], u_rsem.at[at])

    def substitute(half):
        chosen = halves[half]

        def forward(i, carry):
            _, low, _ = geometry(i)
            new = []
            for g, before in zip(chosen, carry):
                here = rows_of(g)
                now = inv[i, here, :] * (rhs[i, here, :] + low * before)
                rhs[i, here, :] = now
                new.append(now)
            return tuple(new)

        def backward(n, carry):
            i = rows - 1 - n
            _, _, high = geometry(i)
            new = []
            for g, after in zip(chosen, carry):
                here = rows_of(g)
                now = rhs[i, here, :] + (high * inv[i, here, :]) * after
                part[i, here, :] = now
                new.append(now)
            return tuple(new)

        zero = tuple(jnp.zeros((SUB, axial), jnp.float32) for _ in chosen)
        lax.fori_loop(0, rows, forward, zero, unroll=4)
        lax.fori_loop(0, rows, backward, zero, unroll=4)

    def reduced_factors(half):
        beta = None
        for s in range(segments):
            v_first, v_last, w_last = [coef_in[s, slot, half] for slot in range(3)]
            w_first = v_last * ((segments + s + 1.0) / (segments + s))
            if s == 0:
                beta = w_last
                factor[half, s, 3] = beta
                continue
            scale = 1.0 / (1.0 - v_first * beta)
            q = scale * w_first
            cross = v_last * beta
            beta = w_last + cross * q
            for slot, plane in enumerate((scale, scale * v_first, q, beta, cross)):
                factor[half, s, slot] = plane

    def reduced_solve(sweep, half):
        firsts, lasts = [], []
        for s in range(segments):
            end = [u_in[sweep, half, s, slot] for slot in range(2)]
            u_first = end[0] * (segments / (stiffness * (segments + s)))
            u_last = end[1] * (segments / (stiffness * (segments + s + 1)))
            if s == 0:
                firsts.append(u_first)
                lasts.append(u_last)
                continue
            p = factor[half, s, 0] * u_first + factor[half, s, 1] * lasts[s - 1]
            firsts.append(p)
            lasts.append(
                u_last + coef_in[s, 1, half] * lasts[s - 1] + factor[half, s, 4] * p
            )
        beyond = jnp.zeros((tile_rows, LANES), jnp.float32)
        ret_out[sweep, half, 0, 0] = beyond
        for s in range(segments - 1, -1, -1):
            ret_out[sweep, half, s, 1] = beyond
            if s < segments - 1:
                ret_out[sweep, half, s + 1, 0] = lasts[s] + factor[half, s, 3] * beyond
            if s > 0:
                beyond = firsts[s] + factor[half, s, 2] * beyond

    def send_back(sweep, half):
        at = (sweep, half)
        copies = sends(ret_out.at[at], ret_in.at[at], ret_ssem.at[at], ret_rsem.at[at])
        for copy in copies:
            copy.start()
        ret_in[sweep, half, seg] = ret_out[sweep, half, seg]
        return copies

    def ends(sweep, half):
        at = (sweep, half)
        await_from(ret_out.at[at], ret_in.at[at], ret_ssem.at[at], ret_rsem.at[at])
        for owner, where_rows, cols in pieces():
            side_a[half, where_rows, cols] = ret_in[sweep, half, owner, 0]
            side_b[half, where_rows, cols] = ret_in[sweep, half, owner, 1]
        return [
            (side_a[half, rows_of(n), :], side_b[half, rows_of(n), :])
            for n in range(len(halves[half]))
        ]

    def solved(i, half, sides):
        for g, (a, b) in zip(halves[half], sides):
            here = rows_of(g)
            yield g, part[i, here, :] + qa[i, here, :] * a + rb[i, here, :] * b

    for copy in halos:
        copy.wait_recv()
    started = [coef_sends, halos]
    for half in (1, 0):
        right_side(0, half)
        started.append(send_ends(0, half))
    await_from(coef_out, coef_in, coef_ssem, coef_rsem)
    for half in (1, 0):
        reduced_factors(half)
        await_ends(0, half)
        reduced_solve(0, half)
        started.append(send_back(0, half))
        substitute(half)

    last_lane = lax.broadcasted_iota(jnp.int32, (width, axial), 1) == axial - 1

    def slope(i, carry):
        here = heat[i]
        rise = jnp.where(last_lane, 0.0, pltpu.roll(here, axial - 1, 1) - here)
        heat[i] = slope_weight * rise - size[i]
        return carry

    for half in (1, 0):
        sides = ends(0, half)

        def advance(i, carry):
            for g, x in solved(i, half, sides):
                state[i, rows_of(g), :] = x
                if g == groups - 1:
                    halo_out[1, 0, pl.ds(i, 1), :] = x[SUB - 1 : SUB, :]
                if g == 0:
                    halo_out[1, 1, pl.ds(i, 1), :] = x[0:1, :]
            return carry

        lax.fori_loop(0, rows, advance, 0, unroll=4)
        if half == 1:
            halos = halo_copies(1)
            started.append(halos)
            for copy in halos:
                copy.start()

    stores = []

    def finish_half(half):
        sides = ends(1, half)

        def finish(i, carry):
            for g, x in solved(i, half, sides):
                here = rows_of(g)
                out_x[i, here, :] = x
                out_s[i, here, :] = x * heat[i, here, :]
            return carry

        lax.fori_loop(0, rows, finish, 0, unroll=4)
        for g in halves[half]:
            here = pl.ds(g * SUB, SUB)
            for m, (src, dst) in enumerate(((out_x, adjoint_hbm), (out_s, sens_hbm))):
                store = pltpu.make_async_copy(
                    src.at[:, here], dst.at[:, here], out_sem.at[m, g]
                )
                store.start()
                stores.append(store)

    def answer(half):
        await_ends(1, half)
        reduced_solve(1, half)
        started.append(send_back(1, half))

    right_side(1, 0)
    started.append(send_ends(1, 0))
    lax.fori_loop(0, rows, slope, 0, unroll=4)
    answer(0)
    for copy in halos:
        copy.wait_recv()
    right_side(1, 1)
    started.append(send_ends(1, 1))
    substitute(0)
    substitute(1)
    finish_half(0)
    answer(1)
    finish_half(1)

    for copies in started:
        for copy in copies:
            copy.wait_send()
    for store in stores:
        store.wait()


def deliver(adjoint, sens, adjoint_out, sens_out, sem):
    parts = sem.shape[1]
    span = adjoint.shape[0] // parts
    copies = []
    for n in range(parts):
        at = pl.ds(n * span, span)
        for m, (src, dst) in enumerate(((adjoint, adjoint_out), (sens, sens_out))):
            copies.append(pltpu.make_async_copy(src.at[at], dst.at[at], sem.at[m, n]))
    for copy in copies:
        copy.start()
    for copy in copies:
        copy.wait()


def solution(mesh):
    segments, sectors = mesh.shape["rad"], mesh.shape["azi"]
    spec = P("rad", "azi", None)

    def body(heat, size, flux, goal, start):
        rows, width, axial = heat.shape
        half_rows = width // 2
        tile_rows = half_rows * axial // (segments * LANES)
        block = pltpu.VMEM((rows, width, axial), jnp.float32)
        tile = (tile_rows, LANES)
        shape = jax.ShapeDtypeStruct((rows, width, axial), jnp.float32)
        dma = pltpu.SemaphoreType.DMA
        cells = rows * width * axial
        adjoint, sens = pl.pallas_call(
            functools.partial(kernel, segments, sectors),
            out_shape=(shape, shape),
            in_specs=[pl.BlockSpec(memory_space=pltpu.HBM)] * 5,
            out_specs=[pl.BlockSpec(memory_space=pl.ANY)] * 2,
            scratch_shapes=[block] * 12
            + [
                pltpu.VMEM((2, 2, rows, axial), jnp.float32),
                pltpu.VMEM((2, 2, rows, axial), jnp.float32),
                pltpu.VMEM((segments, 3, 2) + tile, jnp.float32),
                pltpu.VMEM((segments, 3, 2) + tile, jnp.float32),
                pltpu.VMEM((2, 2, segments, 2) + tile, jnp.float32),
                pltpu.VMEM((2, 2, segments, 2) + tile, jnp.float32),
                pltpu.VMEM((2, 2, segments, 2) + tile, jnp.float32),
                pltpu.VMEM((2, 2, segments, 2) + tile, jnp.float32),
                pltpu.VMEM((2, segments, 5) + tile, jnp.float32),
                pltpu.VMEM((2, half_rows, axial), jnp.float32),
                pltpu.VMEM((2, half_rows, axial), jnp.float32),
                dma((5, 2)),
                dma((2, width // SUB)),
                dma((2, 2)),
                dma((2, 2)),
                dma((segments,)),
                dma((segments,)),
                dma((2, 2, segments)),
                dma((2, 2, segments)),
                dma((2, 2, segments)),
                dma((2, 2, segments)),
            ],
            compiler_params=pltpu.CompilerParams(
                collective_id=0, has_side_effects=True, vmem_limit_bytes=51 * 2**20
            ),
            cost_estimate=pl.CostEstimate(
                flops=120 * cells, bytes_accessed=28 * cells, transcendentals=2 * cells
            ),
        )(heat, size, flux, goal, start)
        return pl.pallas_call(
            deliver,
            out_shape=(shape, shape),
            in_specs=[pl.BlockSpec(memory_space=pl.ANY)] * 2,
            out_specs=[pl.BlockSpec(memory_space=pl.ANY)] * 2,
            scratch_shapes=[dma((2, 4))],
            compiler_params=pltpu.CompilerParams(vmem_limit_bytes=2**20),
            cost_estimate=pl.CostEstimate(
                flops=0, bytes_accessed=16 * cells, transcendentals=0
            ),
        )(adjoint, sens)

    return jax.shard_map(
        body, mesh=mesh, in_specs=(spec,) * 5, out_specs=(spec, spec), check_vma=False
    )
```

```python
import functools

import jax
import jax.numpy as jnp
from jax import lax
from jax.experimental import pallas as pl
from jax.experimental.pallas import tpu as pltpu
from jax.sharding import PartitionSpec as P

radial_weight = 8.0
azimuth_weight = 0.25
axial_weight = 0.25
flow_weight = 0.5
mass_weight = 1.0
heat_weight = 0.25
arrhenius_exponent = 2.0
slope_weight = 2.0

MESH = pl.DeviceIdType.MESH
LANES = 128
SUB = 8


def kernel(
    segments,
    sectors,
    heat_hbm,
    size_hbm,
    flux_hbm,
    goal_hbm,
    start_hbm,
    out_x,
    out_s,
    heat,
    size,
    flux,
    goal,
    state,
    inv,
    qa,
    rb,
    rhs,
    part,
    halo_out,
    halo_in,
    coef_out,
    coef_in,
    u_out,
    u_in,
    ret_out,
    ret_in,
    factor,
    side_a,
    side_b,
    in_sem,
    halo_ssem,
    halo_rsem,
    coef_ssem,
    coef_rsem,
    u_ssem,
    u_rsem,
    ret_ssem,
    ret_rsem,
):
    rows, width, axial = heat.shape
    groups = width // SUB
    chunks = axial // LANES
    per_chunk = segments // chunks
    tile_rows = width // (2 * per_chunk)
    inner, outer = tuple(range(1, groups - 1)), (0, groups - 1)
    halves = (inner, outer)
    total = rows * segments
    stiffness = radial_weight * rows * rows

    seg = lax.axis_index("rad")
    sec = lax.axis_index("azi")
    above = lax.rem(sec + 1, sectors)
    below = lax.rem(sec + sectors - 1, sectors)
    peers = [lax.rem(seg + k, segments) for k in range(1, segments)]
    first = seg * rows

    span = rows // 2
    loads = [
        [
            pltpu.make_async_copy(
                src.at[pl.ds(part_of * span, span)],
                dst.at[pl.ds(part_of * span, span)],
                in_sem.at[n, part_of],
            )
            for part_of in range(2)
        ]
        for n, (src, dst) in enumerate(
            (
                (start_hbm, state),
                (heat_hbm, heat),
                (size_hbm, size),
                (flux_hbm, flux),
                (goal_hbm, goal),
            )
        )
    ]
    for load in loads:
        for copy in load:
            copy.start()

    def await_load(load):
        for copy in load:
            copy.wait()

    barrier = pltpu.get_barrier_semaphore()
    for peer in peers:
        pl.semaphore_signal(barrier, inc=1, device_id=(peer, sec), device_id_type=MESH)
    for near in (above, below):
        pl.semaphore_signal(barrier, inc=1, device_id=(seg, near), device_id_type=MESH)

    def halo_copies(sweep):
        return [
            pltpu.make_async_remote_copy(
                src_ref=halo_out.at[sweep, side],
                dst_ref=halo_in.at[sweep, side],
                send_sem=halo_ssem.at[sweep, side],
                recv_sem=halo_rsem.at[sweep, side],
                device_id=(seg, near),
                device_id_type=MESH,
            )
            for side, near in ((0, above), (1, below))
        ]

    def sends(src, dst, ssem, rsem):
        return [
            pltpu.make_async_remote_copy(
                src_ref=src.at[peer],
                dst_ref=dst.at[seg],
                send_sem=ssem.at[peer],
                recv_sem=rsem.at[seg],
                device_id=(peer, sec),
                device_id_type=MESH,
            )
            for peer in peers
        ]

    def await_from(src, dst, ssem, rsem):
        for peer in peers:
            pltpu.make_async_remote_copy(
                src_ref=src.at[peer],
                dst_ref=dst.at[peer],
                send_sem=ssem.at[peer],
                recv_sem=rsem.at[peer],
                device_id=(peer, sec),
                device_id_type=MESH,
            ).wait_recv()

    def geometry(i):
        row = (first + i).astype(jnp.float32)
        radius = 1.0 + (row + 0.5) * (1.0 / total)
        low = stiffness * (1.0 + row * (1.0 / total))
        high = stiffness * (1.0 + (row + 1.0) * (1.0 / total))
        return radius, low, high

    def azimuth_coef(radius):
        return azimuth_weight / jnp.full((1, LANES), radius, jnp.float32)

    def wide(line):
        return jnp.concatenate([line] * chunks, axis=1)

    await_load(loads[0])

    def pack(i, carry):
        halo_out[0, 0, pl.ds(i, 1), :] = state[i, width - 1 : width, :]
        halo_out[0, 1, pl.ds(i, 1), :] = state[i, 0:1, :]
        return carry

    lax.fori_loop(0, rows, pack, 0, unroll=4)
    pl.semaphore_wait(barrier, segments + 1)
    halos = halo_copies(0)
    for copy in halos:
        copy.start()

    for load in loads[1:4]:
        await_load(load)

    def rows_of(g):
        return slice(g * SUB, (g + 1) * SUB)

    def pieces():
        for c in range(chunks):
            for k in range(per_chunk):
                where_rows = slice(k * tile_rows, (k + 1) * tile_rows)
                where_cols = slice(c * LANES, (c + 1) * LANES)
                yield c * per_chunk + k, where_rows, where_cols

    def scatter(slot, plane, c_first, c_last):
        for n, chosen in enumerate(halves):
            lines = jnp.concatenate([plane[rows_of(g)] for g in chosen], axis=0)
            for owner, where_rows, cols in pieces():
                if c_first * LANES <= cols.start < c_last * LANES:
                    at = cols.start - c_first * LANES
                    coef_out[owner, slot, n] = lines[where_rows, at : at + LANES]

    half = 2 * LANES
    for h in range(axial // half):
        cols = slice(h * half, (h + 1) * half)

        def eliminate(i, carry):
            ratio, ea, prod, va, _ = carry
            radius, low, high = geometry(i)
            az2 = 2.0 * azimuth_coef(radius)
            az2 = jnp.concatenate([az2, az2], axis=1)
            viscosity = jnp.exp(
                arrhenius_exponent - arrhenius_exponent * heat[i, :, cols]
            )
            extent = size[i, :, cols]
            shear = (heat_weight * arrhenius_exponent) * viscosity * extent
            ahead = radius * (axial_weight + flow_weight * flux[i, :, cols])
            excess = (
                ahead + radius * (shear * extent + (mass_weight + axial_weight)) + az2
            )
            top = low * ratio + excess
            inverse = 1.0 / (top + high)
            ratio = top * inverse
            ea = (low * inverse) * ea
            upper = high * inverse
            va = va + prod * ea
            prod = prod * upper
            flux[i, :, cols] = ahead
            size[i, :, cols] = shear
            inv[i, :, cols] = inverse
            qa[i, :, cols] = ea
            return ratio, ea, prod, va, upper

        one = jnp.ones((width, half), jnp.float32)
        zero = jnp.zeros((width, half), jnp.float32)
        _, ea, _, va, upper = lax.fori_loop(
            0, rows, eliminate, (one, one, one, zero, zero), unroll=4
        )
        scatter(0, va, 2 * h, 2 * h + 2)
        scatter(1, ea, 2 * h, 2 * h + 2)
        scatter(2, upper, 2 * h, 2 * h + 2)

    coef_sends = sends(coef_out, coef_in, coef_ssem, coef_rsem)
    for copy in coef_sends:
        copy.start()
    coef_in[seg] = coef_out[seg]

    def respond(n, carry):
        q_next, r_next = carry
        i = rows - 1 - n
        _, _, high = geometry(i)
        upper = high * inv[i]
        q_next = qa[i] + upper * q_next
        r_next = upper * r_next
        qa[i] = q_next
        rb[i] = r_next
        return q_next, r_next

    lax.fori_loop(
        0,
        rows,
        respond,
        (jnp.zeros((width, axial), jnp.float32), jnp.ones((width, axial), jnp.float32)),
        unroll=4,
    )

    await_load(loads[4])
    sub = lax.broadcasted_iota(jnp.int32, (SUB, axial), 0)
    lane = lax.broadcasted_iota(jnp.int32, (SUB, axial), 1)

    def right_side(sweep, half):
        chosen = halves[half]

        def step(i, carry):
            radius, _, _ = geometry(i)
            az = wide(azimuth_coef(radius))
            rolled_up, rolled_down, new = {}, {}, []

            def block(g):
                return state[i, g * SUB : (g + 1) * SUB, :]

            def up(g):
                if g < 0:
                    return jnp.broadcast_to(
                        halo_in[sweep, 0, pl.ds(i, 1), :], (SUB, axial)
                    )
                if g not in rolled_up:
                    rolled_up[g] = pltpu.roll(block(g), 1, 0)
                return rolled_up[g]

            def down(g):
                if g >= groups:
                    return jnp.broadcast_to(
                        halo_in[sweep, 1, pl.ds(i, 1), :], (SUB, axial)
                    )
                if g not in rolled_down:
                    rolled_down[g] = pltpu.roll(block(g), SUB - 1, 0)
                return rolled_down[g]

            for g, (u_first, u_last) in zip(chosen, carry):
                here = slice(g * SUB, (g + 1) * SUB)
                x = block(g)
                sides = jnp.where(sub == 0, up(g - 1), up(g)) + jnp.where(
                    sub == SUB - 1, down(g + 1), down(g)
                )
                before = jnp.where(lane == 0, 0.0, pltpu.roll(x, 1, 1))
                after = jnp.where(lane == axial - 1, 0.0, pltpu.roll(x, axial - 1, 1))
                value = (
                    radius * (goal[i, here, :] + mass_weight * x + axial_weight * before)
                    + flux[i, here, :] * after
                    + az * sides
                )
                rhs[i, here, :] = value
                new.append(
                    (u_first + qa[i, here, :] * value, u_last + rb[i, here, :] * value)
                )
            return tuple(new)

        zero = jnp.zeros((SUB, axial), jnp.float32)
        sums = lax.fori_loop(0, rows, step, tuple((zero, zero) for _ in chosen), unroll=2)
        for slot in range(2):
            lines = jnp.concatenate([pair[slot] for pair in sums], axis=0)
            for owner, where_rows, cols in pieces():
                u_out[sweep, half, owner, slot] = lines[where_rows, cols]

    def send_ends(sweep, half):
        at = (sweep, half)
        copies = sends(u_out.at[at], u_in.at[at], u_ssem.at[at], u_rsem.at[at])
        for copy in copies:
            copy.start()
        u_in[sweep, half, seg] = u_out[sweep, half, seg]
        return copies

    def await_ends(sweep, half):
        at = (sweep, half)
        await_from(u_out.at[at], u_in.at[at], u_ssem.at[at], u_rsem.at[at])

    def substitute(half):
        chosen = halves[half]

        def forward(i, carry):
            _, low, _ = geometry(i)
            new = []
            for g, before in zip(chosen, carry):
                here = rows_of(g)
                now = inv[i, here, :] * (rhs[i, here, :] + low * before)
                rhs[i, here, :] = now
                new.append(now)
            return tuple(new)

        def backward(n, carry):
            i = rows - 1 - n
            _, _, high = geometry(i)
            new = []
            for g, after in zip(chosen, carry):
                here = rows_of(g)
                now = rhs[i, here, :] + (high * inv[i, here, :]) * after
                part[i, here, :] = now
                new.append(now)
            return tuple(new)

        zero = tuple(jnp.zeros((SUB, axial), jnp.float32) for _ in chosen)
        lax.fori_loop(0, rows, forward, zero, unroll=4)
        lax.fori_loop(0, rows, backward, zero, unroll=4)

    def reduced_factors(half):
        beta = None
        for s in range(segments):
            v_first, v_last, w_last = [coef_in[s, slot, half] for slot in range(3)]
            w_first = v_last * ((segments + s + 1.0) / (segments + s))
            if s == 0:
                beta = w_last
                factor[half, s, 3] = beta
                continue
            scale = 1.0 / (1.0 - v_first * beta)
            q = scale * w_first
            cross = v_last * beta
            beta = w_last + cross * q
            for slot, plane in enumerate((scale, scale * v_first, q, beta, cross)):
                factor[half, s, slot] = plane

    def reduced_solve(sweep, half):
        firsts, lasts = [], []
        for s in range(segments):
            end = [u_in[sweep, half, s, slot] for slot in range(2)]
            u_first = end[0] * (segments / (stiffness * (segments + s)))
            u_last = end[1] * (segments / (stiffness * (segments + s + 1)))
            if s == 0:
                firsts.append(u_first)
                lasts.append(u_last)
                continue
            p = factor[half, s, 0] * u_first + factor[half, s, 1] * lasts[s - 1]
            firsts.append(p)
            lasts.append(
                u_last + coef_in[s, 1, half] * lasts[s - 1] + factor[half, s, 4] * p
            )
        beyond = jnp.zeros((tile_rows, LANES), jnp.float32)
        ret_out[sweep, half, 0, 0] = beyond
        for s in range(segments - 1, -1, -1):
            ret_out[sweep, half, s, 1] = beyond
            if s < segments - 1:
                ret_out[sweep, half, s + 1, 0] = lasts[s] + factor[half, s, 3] * beyond
            if s > 0:
                beyond = firsts[s] + factor[half, s, 2] * beyond

    def send_back(sweep, half):
        at = (sweep, half)
        copies = sends(ret_out.at[at], ret_in.at[at], ret_ssem.at[at], ret_rsem.at[at])
        for copy in copies:
            copy.start()
        ret_in[sweep, half, seg] = ret_out[sweep, half, seg]
        return copies

    def ends(sweep, half):
        at = (sweep, half)
        await_from(ret_out.at[at], ret_in.at[at], ret_ssem.at[at], ret_rsem.at[at])
        for owner, where_rows, cols in pieces():
            side_a[half, where_rows, cols] = ret_in[sweep, half, owner, 0]
            side_b[half, where_rows, cols] = ret_in[sweep, half, owner, 1]
        return [
            (side_a[half, rows_of(n), :], side_b[half, rows_of(n), :])
            for n in range(len(halves[half]))
        ]

    def solved(i, half, sides):
        for g, (a, b) in zip(halves[half], sides):
            here = rows_of(g)
            yield g, part[i, here, :] + qa[i, here, :] * a + rb[i, here, :] * b

    for copy in halos:
        copy.wait_recv()
    started = [coef_sends, halos]
    for half in (1, 0):
        right_side(0, half)
        started.append(send_ends(0, half))
    await_from(coef_out, coef_in, coef_ssem, coef_rsem)
    for half in (1, 0):
        reduced_factors(half)
    for half in (1, 0):
        substitute(half)
        await_ends(0, half)
        reduced_solve(0, half)
        started.append(send_back(0, half))

    last_lane = lax.broadcasted_iota(jnp.int32, (width, axial), 1) == axial - 1

    def slope(i, carry):
        here = heat[i]
        rise = jnp.where(last_lane, 0.0, pltpu.roll(here, axial - 1, 1) - here)
        heat[i] = slope_weight * rise - size[i]
        return carry

    lax.fori_loop(0, rows, slope, 0, unroll=4)

    for half in (1, 0):
        sides = ends(0, half)

        def advance(i, carry):
            for g, x in solved(i, half, sides):
                state[i, rows_of(g), :] = x
                if g == groups - 1:
                    halo_out[1, 0, pl.ds(i, 1), :] = x[SUB - 1 : SUB, :]
                if g == 0:
                    halo_out[1, 1, pl.ds(i, 1), :] = x[0:1, :]
            return carry

        lax.fori_loop(0, rows, advance, 0, unroll=4)
        if half == 1:
            halos = halo_copies(1)
            started.append(halos)
            for copy in halos:
                copy.start()

    for half in (0, 1):
        if half == 1:
            for copy in halos:
                copy.wait_recv()
        right_side(1, half)
        started.append(send_ends(1, half))
    for half in (0, 1):
        substitute(half)
        await_ends(1, half)
        reduced_solve(1, half)
        started.append(send_back(1, half))

    for half in (0, 1):
        sides = ends(1, half)

        def finish(i, carry):
            for g, x in solved(i, half, sides):
                here = rows_of(g)
                out_x[i, here, :] = x
                out_s[i, here, :] = x * heat[i, here, :]
            return carry

        lax.fori_loop(0, rows, finish, 0, unroll=4)
    for copies in started:
        for copy in copies:
            copy.wait_send()


def deliver(adjoint, sens, adjoint_out, sens_out, sem):
    parts = sem.shape[1]
    span = adjoint.shape[0] // parts
    copies = []
    for n in range(parts):
        at = pl.ds(n * span, span)
        for m, (src, dst) in enumerate(((adjoint, adjoint_out), (sens, sens_out))):
            copies.append(pltpu.make_async_copy(src.at[at], dst.at[at], sem.at[m, n]))
    for copy in copies:
        copy.start()
    for copy in copies:
        copy.wait()


def solution(mesh):
    segments, sectors = mesh.shape["rad"], mesh.shape["azi"]
    spec = P("rad", "azi", None)

    def body(heat, size, flux, goal, start):
        rows, width, axial = heat.shape
        half_rows = width // 2
        tile_rows = half_rows * axial // (segments * LANES)
        block = pltpu.VMEM((rows, width, axial), jnp.float32)
        tile = (tile_rows, LANES)
        shape = jax.ShapeDtypeStruct((rows, width, axial), jnp.float32)
        dma = pltpu.SemaphoreType.DMA
        cells = rows * width * axial
        adjoint, sens = pl.pallas_call(
            functools.partial(kernel, segments, sectors),
            out_shape=(shape, shape),
            in_specs=[pl.BlockSpec(memory_space=pltpu.HBM)] * 5,
            out_specs=[pl.BlockSpec(memory_space=pltpu.VMEM)] * 2,
            scratch_shapes=[block] * 10
            + [
                pltpu.VMEM((2, 2, rows, axial), jnp.float32),
                pltpu.VMEM((2, 2, rows, axial), jnp.float32),
                pltpu.VMEM((segments, 3, 2) + tile, jnp.float32),
                pltpu.VMEM((segments, 3, 2) + tile, jnp.float32),
                pltpu.VMEM((2, 2, segments, 2) + tile, jnp.float32),
                pltpu.VMEM((2, 2, segments, 2) + tile, jnp.float32),
                pltpu.VMEM((2, 2, segments, 2) + tile, jnp.float32),
                pltpu.VMEM((2, 2, segments, 2) + tile, jnp.float32),
                pltpu.VMEM((2, segments, 5) + tile, jnp.float32),
                pltpu.VMEM((2, half_rows, axial), jnp.float32),
                pltpu.VMEM((2, half_rows, axial), jnp.float32),
                dma((5, 2)),
                dma((2, 2)),
                dma((2, 2)),
                dma((segments,)),
                dma((segments,)),
                dma((2, 2, segments)),
                dma((2, 2, segments)),
                dma((2, 2, segments)),
                dma((2, 2, segments)),
            ],
            compiler_params=pltpu.CompilerParams(
                collective_id=0, has_side_effects=True, vmem_limit_bytes=51 * 2**20
            ),
            cost_estimate=pl.CostEstimate(
                flops=120 * cells, bytes_accessed=28 * cells, transcendentals=2 * cells
            ),
        )(heat, size, flux, goal, start)
        return pl.pallas_call(
            deliver,
            out_shape=(shape, shape),
            in_specs=[pl.BlockSpec(memory_space=pl.ANY)] * 2,
            out_specs=[pl.BlockSpec(memory_space=pl.ANY)] * 2,
            scratch_shapes=[dma((2, 4))],
            compiler_params=pltpu.CompilerParams(vmem_limit_bytes=2**20),
            cost_estimate=pl.CostEstimate(
                flops=0, bytes_accessed=16 * cells, transcendentals=0
            ),
        )(adjoint, sens)

    return jax.shard_map(
        body, mesh=mesh, in_specs=(spec,) * 5, out_specs=(spec, spec), check_vma=False
    )
```
